128 devices in a mesh: tracer: 8 (over y, x_lo), domain: 16 (over x_hi, z, core).
Axes of the slice: x: 4 (x_hi: 2, x_lo: 2; x = x_hi * 2 + x_lo), y: 4, z: 4, core: 2. Of those that a mesh axis runs over, the one named last changes fastest.
Arguments:
- log_rate: float32 [256, 256, 256], P('domain'), may hold values from -1.6 to 0
- velocity: float32 [256, 256], replicated, may hold values from 0.2 to 1
- initial: float32 [8, 256, 256, 256], P('tracer', 'domain'), may hold values from -6 to 6
- profile: float32 [8, 256, 256], P('tracer'), may hold values from 0.5 to 4
- plane: int32 [8], P('tracer'), may hold values from 0 to 255
- depth: int32 [8, 32768], P('tracer'), may hold values from 0 to 255
- row: int32 [8, 32768], P('tracer'), may hold values from 0 to 255
- column: int32 [8, 32768], P('tracer'), may hold values from 0 to 255
- step_of: int32 [8, 32768], P('tracer'), may hold values from 1 to 2
- observed: float32 [8, 32768], P('tracer'), may hold values from -6 to 6
Outputs:
- smoothed_gradient: float32 [128, 128, 128], P('domain', 'tracer')
The draws below stay inside these ranges and needn't reach their ends.
All inputs are finite; a program needn't handle non-finite values.
Results may differ from the reference program's by a relative error of at most 0.0003.
Values sent between devices are 32-bit elements; how exact they have to be, the bound alone decides.
No kernel may reach another device: no remote copies, remote signals or barrier semaphores. Data moves between devices by JAX's collectives and lax.ppermute only.
A program may use at most 512 MiB of HBM per device.

```python
import functools
import math
import jax
import jax.numpy as jnp
from jax import lax

R = 2
STEPS = 2
PROBES = 32768
FX = 256
FY = 256
FZ = 256
TRACERS = 8


def with_ends(values, stream_key, smallest, top_value):
    longest = values.shape.index(max(values.shape))
    spots = []
    for shift in (0, 1):
        where = [jax.random.randint(jax.random.fold_in(stream_key, axis), (), 0, length) for axis, length in enumerate(values.shape)]
        where[longest] = (where[longest] + shift) % values.shape[longest]
        spots.append(tuple(where))
    return values.at[spots[0]].set(smallest).at[spots[1]].set(top_value)


def block_levels(stream_key, shape, split, least, high):
    def one(axis_at, blocks):
        draws = jax.random.uniform(jax.random.fold_in(jax.random.fold_in(stream_key, 6), axis_at), (blocks,), jnp.float32, least / len(split), high / len(split))
        return jnp.repeat(jnp.exp(draws), shape[axis_at] // blocks).reshape((-1,) + (1,) * (len(shape) - axis_at - 1))

    factor_of = one(*split[0])
    for cut in split[1:]:
        factor_of = factor_of * one(*cut)
    return factor_of


def noise(own_key, dims, width, limit, split=(), kind=jnp.bfloat16):
    values = width * jax.random.normal(own_key, dims, jnp.float32)
    if split:
        values = values * block_levels(own_key, dims, split, -0.22, 0.18)
    return jnp.clip(values, -limit, limit).astype(kind)


def setup_inputs(seed: int = 0) -> dict:
    arg_keys = jax.random.split(jax.random.key(seed), 11)
    return {
        "log_rate": jnp.clip(-1.6 + 1.6 * jax.random.uniform(arg_keys[0], (FZ, FX, FY), jnp.float32) ** block_levels(arg_keys[0], (FZ, FX, FY), ((0, 16),), -0.2, 0.2), -1.6, 0.0),
        "velocity": jnp.clip(jax.random.uniform(arg_keys[1], (FX, FY), jnp.float32, 0.2, 1.0), 0.2, 1.0),
        "initial": noise(arg_keys[2], (TRACERS, FZ, FX, FY), 1.0, 6.0, ((0, 8), (1, 16)), jnp.float32),
        "profile": jnp.clip(jnp.exp(math.log(4.0) - 2.0794415 * jax.random.uniform(arg_keys[3], (TRACERS, FX, FY), jnp.float32) ** block_levels(arg_keys[3], (TRACERS, FX, FY), ((0, 8),), -0.2, 0.2)), 0.5, 4.0),
        "plane": with_ends(jax.random.randint(arg_keys[4], (TRACERS,), 0, FZ), jax.random.fold_in(arg_keys[4], 1), 0, FZ - 1).astype(jnp.int32),
        "depth": with_ends(jax.random.randint(arg_keys[5], (TRACERS, PROBES), 0, FZ), jax.random.fold_in(arg_keys[5], 1), 0, FZ - 1).astype(jnp.int32),
        "row": with_ends(jax.random.randint(arg_keys[6], (TRACERS, PROBES), 0, FX), jax.random.fold_in(arg_keys[6], 1), 0, FX - 1).astype(jnp.int32),
        "column": with_ends(jax.random.randint(arg_keys[7], (TRACERS, PROBES), 0, FY), jax.random.fold_in(arg_keys[7], 1), 0, FY - 1).astype(jnp.int32),
        "step_of": with_ends(jax.random.randint(arg_keys[8], (TRACERS, PROBES), 1, STEPS + 1), jax.random.fold_in(arg_keys[8], 1), 1, STEPS).astype(jnp.int32),
        "observed": noise(arg_keys[9], (TRACERS, PROBES), 1.0, 6.0, ((0, 8),), jnp.float32),
    }


TIME_STEP = 0.14
PRIOR_RANGE = 4.0


def face_rates(kappa_field):
    return [0.5 * (kappa_field + jnp.roll(kappa_field, -1, axis_dim)) for axis_dim in range(3)]


def diffusion(values, faces):
    result = jnp.zeros_like(values)
    for axis_dim in range(3):
        ahead_cell = jnp.roll(values, -1, axis_dim)
        behind_cell = jnp.roll(values, 1, axis_dim)
        result = result + faces[axis_dim] * (ahead_cell - values) - jnp.roll(faces[axis_dim], 1, axis_dim) * (values - behind_cell)
    return result


def sensitivity(state, adjoint):
    result = jnp.zeros_like(state)
    for axis_dim in range(3):
        product = (jnp.roll(state, -1, axis_dim) - state) * (jnp.roll(adjoint, -1, axis_dim) - adjoint)
        result = result + product + jnp.roll(product, 1, axis_dim)
    return -0.5 * result


def one_tracer(kappa_field, faces, velocity, items):
    initial, profile, plane, depth, row, column, step_of, observed = items
    depth_count, rows_count, cols_count = initial.shape
    layers = lax.iota(jnp.int32, depth_count)
    source = jnp.where((layers == plane)[:, None, None], profile[None], 0.0)
    wind = velocity[None]
    flat = depth * (rows_count * cols_count) + row * cols_count + column
    states = []
    values = initial
    sampled = jnp.zeros_like(observed)
    for section in range(STEPS):
        states.append(values)
        values = values + TIME_STEP * (diffusion(values, faces) - wind * (values - jnp.roll(values, 1, 0))) + TIME_STEP * source
        sampled = jnp.where(step_of == section + 1, values.reshape(-1)[flat], sampled)
    residual = sampled - observed

    def inject(section):
        empty = jnp.zeros((depth_count * rows_count * cols_count,), initial.dtype)
        return empty.at[flat].add(jnp.where(step_of == section, residual, 0.0)).reshape(initial.shape)

    adjoint = inject(STEPS)
    gradient = jnp.zeros_like(initial)
    for section in reversed(range(STEPS)):
        gradient = gradient + sensitivity(states[section], adjoint)
        if section > 0:
            adjoint = adjoint + TIME_STEP * (diffusion(adjoint, faces) - wind * (adjoint - jnp.roll(adjoint, -1, 0))) + inject(section)
    fine_grad = TIME_STEP * kappa_field * gradient
    return fine_grad.reshape(depth_count // R, R, rows_count // R, R, cols_count // R, R).sum(axis=(1, 3, 5))


def symbol_of(length):
    angles = (2.0 * math.pi / length) * lax.iota(jnp.float32, length)
    return 2.0 - 2.0 * jnp.cos(angles)


def prior_filter(shape):
    lam_sum = symbol_of(shape[0])[:, None, None] + symbol_of(shape[1])[None, :, None] + symbol_of(shape[2])[None, None, :]
    factor = 1.0 + PRIOR_RANGE * lam_sum
    return 1.0 / (factor * factor)


def reference(log_rate, velocity, initial, profile, plane, depth, row, column, step_of, observed):
    kappa_field = jnp.exp(log_rate)
    faces = face_rates(kappa_field)
    worker = functools.partial(one_tracer, kappa_field, faces, velocity)
    partials = lax.map(worker, (initial, profile, plane, depth, row, column, step_of, observed))
    summed = jnp.sum(partials, axis=0)
    spectrum = jnp.fft.fftn(summed)
    smoothed = jnp.real(jnp.fft.ifftn(spectrum * prior_filter(summed.shape)))
    return smoothed.astype(summed.dtype)
```

```python
import functools
import math

import jax
import jax.numpy as jnp
import numpy as np
from jax import lax
from jax.experimental import pallas as pl
from jax.experimental.pallas import tpu as pltpu
from jax.sharding import PartitionSpec as P

R = 2
STEPS = 2
TIME_STEP = 0.14
PRIOR_RANGE = 4.0

HALO = 4
LEAD = 2
LANES = 128
LONG, SHORT = 8, 4
PAD = 8
STRIP = 32


def hartley(length):
    phases = np.outer(np.arange(length), np.arange(length)) % length
    angles = 2.0 * math.pi / length * phases
    return (np.cos(angles) + np.sin(angles)).astype(np.float32)


def symbol(length):
    return (2.0 - 2.0 * np.cos(2.0 * math.pi / length * np.arange(length))).astype(np.float32)


def sort_kernel(
    offset_ref,
    depth_ref,
    row_ref,
    column_ref,
    step_ref,
    observed_ref,
    keys_out,
    values_out,
    starts_out,
    keys,
    values,
):
    offset = offset_ref[0]
    plane = (depth_ref[...] - (offset - LEAD)) & 255
    key = (plane << 17) | ((step_ref[...] - 1) << 16) | (row_ref[...] << 8) | column_ref[...]
    keys[...] = key.reshape(keys.shape)
    values[...] = observed_ref[...].reshape(values.shape)
    for index in range(starts_out.shape[0]):
        if index == 0:
            starts_out[index] = 0
        else:
            starts_out[index] = jnp.sum((key < (index << 17)).astype(jnp.int32))

    lane = lax.broadcasted_iota(jnp.int32, (8, LANES), 1)
    sublane = lax.broadcasted_iota(jnp.int32, (8, LANES), 0)

    def pair(low, high, down):
        (key_a, value_a), (key_b, value_b) = low, high
        if down is False:
            swap = key_a > key_b
        elif down is True:
            swap = key_a < key_b
        else:
            swap = jnp.logical_xor(key_a > key_b, down)
        return (
            (jnp.where(swap, key_b, key_a), jnp.where(swap, value_b, value_a)),
            (jnp.where(swap, key_a, key_b), jnp.where(swap, value_a, value_b)),
        )

    def within(item, axis, distance, upper, largest):
        key, value = item
        size = key.shape[axis]
        key_p = jnp.where(
            upper, pltpu.roll(key, distance, axis), pltpu.roll(key, size - distance, axis)
        )
        value_p = jnp.where(
            upper, pltpu.roll(value, distance, axis), pltpu.roll(value, size - distance, axis)
        )
        gap = key_p - key
        take = jnp.where(largest, gap, -gap) > 0
        return jnp.where(take, key_p, key), jnp.where(take, value_p, value)

    def bit_of(array, bit):
        return ((array >> bit) & 1) == 1

    def registers(items, level, down):
        for bit in range(level, -1, -1):
            for low in range(16):
                if low & (1 << bit):
                    continue
                high = low | (1 << bit)
                order = down(low) if callable(down) else down
                items[low], items[high] = pair(items[low], items[high], order)
        return items

    def sublanes(items, bit, down):
        upper = bit_of(sublane, bit)
        largest = jnp.logical_xor(upper, down) if not isinstance(down, bool) else (
            jnp.logical_not(upper) if down else upper
        )
        return [within(item, 0, 1 << bit, upper, largest) for item in items]

    def load(group):
        return [(keys[group * 16 + i], values[group * 16 + i]) for i in range(16)]

    def store(group, items):
        for i, (key, value) in enumerate(items):
            keys[group * 16 + i] = key
            values[group * 16 + i] = value

    for group in range(2):
        items = load(group)
        for level in range(1, 4):
            items = registers(
                items, level - 1, lambda low, level=level: bool((low >> level) & 1)
            )
        items = registers(items, 3, bit_of(sublane, 0))
        for level in range(1, 3):
            down = bit_of(sublane, level)
            for bit in range(level - 1, -1, -1):
                items = sublanes(items, bit, down)
            items = registers(items, 3, down)
        down = bool(group)
        for bit in range(2, -1, -1):
            items = sublanes(items, bit, down)
        items = registers(items, 3, down)
        store(group, items)

    def merge(level, carry):
        down = ((lane >> level) & 1) == 1

        def across(turn, inner):
            bit = level - 1 - turn
            distance = jnp.int32(1) << bit
            upper = ((lane >> bit) & 1) == 1
            largest = jnp.logical_xor(upper, down)
            for i in range(32):
                keys[i], values[i] = within((keys[i], values[i]), 1, distance, upper, largest)
            return inner

        lax.fori_loop(0, level, across, 0)
        for i in range(16):
            low, high = pair((keys[i], values[i]), (keys[i + 16], values[i + 16]), down)
            keys[i], values[i] = low
            keys[i + 16], values[i + 16] = high
        for group in range(2):
            items = load(group)
            for bit in range(2, -1, -1):
                items = sublanes(items, bit, down)
            items = registers(items, 3, down)
            store(group, items)
        return carry

    lax.fori_loop(0, 8, merge, 0)

    for half in range(2):
        part = keys[pl.ds(half * 16, 16)].reshape(LANES, LANES)
        keys_out[pl.ds(half, LANES, 2), :] = part.T
        part = values[pl.ds(half * 16, 16)].reshape(LANES, LANES)
        values_out[pl.ds(half, LANES, 2), :] = part.T
    keys_out[2 * LANES :, :] = jnp.full((8, LANES), -1, jnp.int32)
    values_out[2 * LANES :, :] = jnp.zeros((8, LANES), jnp.float32)


def sort_probes(offset, depth, row, column, step_of, observed, planes):
    count = depth.size
    shape = (count // LANES, LANES)
    vmem = pl.BlockSpec(memory_space=pltpu.VMEM)
    smem = pl.BlockSpec(memory_space=pltpu.SMEM)
    return pl.pallas_call(
        sort_kernel,
        out_shape=(
            jax.ShapeDtypeStruct((shape[0] + 8, LANES), jnp.int32),
            jax.ShapeDtypeStruct((shape[0] + 8, LANES), jnp.float32),
            jax.ShapeDtypeStruct((planes + 1,), jnp.int32),
        ),
        in_specs=[smem] + [vmem] * 5,
        out_specs=(vmem, vmem, smem),
        scratch_shapes=[
            pltpu.VMEM((shape[0] // 8, 8, LANES), jnp.int32),
            pltpu.VMEM((shape[0] // 8, 8, LANES), jnp.float32),
        ],
        compiler_params=pltpu.CompilerParams(vmem_limit_bytes=16 * 2**20),
        cost_estimate=pl.CostEstimate(flops=20_000_000, bytes_accessed=2**20, transcendentals=0),
        name="sort_probes",
    )(offset, *(a.reshape(shape) for a in (depth, row, column, step_of, observed)))


def bin_kernel(starts, keys_ref, values_ref, *fields):
    place = pl.program_id(0)
    size = fields[0].shape[1]
    both = STEPS * size
    counts, sums = fields[:STEPS], fields[STEPS:]
    begin, end = starts[place], starts[place + 1]
    first = begin >> 7
    windows = (end - (first << 7) + 2 * LANES - 1) >> 8

    def window(turn):
        at = first + 2 * turn
        key = jnp.concatenate([keys_ref[pl.ds(at, 1), :], keys_ref[pl.ds(at + 1, 1), :]], axis=1)
        value = jnp.concatenate(
            [values_ref[pl.ds(at, 1), :], values_ref[pl.ds(at + 1, 1), :]], axis=1
        )
        target = lax.broadcasted_iota(jnp.int32, (both, 2 * LANES), 0) + (place << 9)
        in_row = jnp.where((key >> 8) == target, 1.0, 0.0).astype(jnp.bfloat16)
        in_column = (key & 255) == lax.broadcasted_iota(jnp.int32, (size, 2 * LANES), 0)
        coarse = value.astype(jnp.bfloat16).astype(jnp.float32)
        rest = value - coarse

        def product(amount):
            return lax.dot_general(
                in_row,
                jnp.where(in_column, amount, 0.0).astype(jnp.bfloat16),
                (((1,), (1,)), ((), ())),
                preferred_element_type=jnp.float32,
            )

        return product(1.0), product(coarse) + product(rest)

    def parts(pair):
        for fields_of, values in zip((counts, sums), pair):
            for step, field in enumerate(fields_of):
                yield field, values[step * size : (step + 1) * size]

    for field, value in parts(window(0)):
        field[0] = value

    def more(turn, carry):
        for field, value in parts(window(turn)):
            field[0] += value
        return carry

    lax.fori_loop(1, windows, more, 0)


def bin_probes(starts, keys, values, rows_count, cols_count):
    places = starts.shape[0] - 1
    vmem = pl.BlockSpec(memory_space=pltpu.VMEM)
    block = pl.BlockSpec((1, rows_count, cols_count), lambda i: (i, 0, 0))
    field = jax.ShapeDtypeStruct((places, rows_count, cols_count), jnp.float32)
    return pl.pallas_call(
        bin_kernel,
        grid=(places,),
        out_shape=(field,) * (2 * STEPS),
        in_specs=[pl.BlockSpec(memory_space=pltpu.SMEM), vmem, vmem],
        out_specs=(block,) * (2 * STEPS),
        compiler_params=pltpu.CompilerParams(
            vmem_limit_bytes=8 * 2**20, dimension_semantics=("arbitrary",)
        ),
        cost_estimate=pl.CostEstimate(
            flops=30_000_000, bytes_accessed=20 * 2**20, transcendentals=0
        ),
        name="bin_probes",
    )(starts, keys, values)


def ahead(parts):
    lane = lax.broadcasted_iota(jnp.int32, parts[0].shape, 1)
    left, right = (pltpu.roll(part, LANES - 1, 1) for part in parts)
    last = lane == LANES - 1
    return jnp.where(last, right, left), jnp.where(last, left, right)


def behind(parts):
    lane = lax.broadcasted_iota(jnp.int32, parts[0].shape, 1)
    left, right = (pltpu.roll(part, 1, 1) for part in parts)
    first = lane == 0
    return jnp.where(first, right, left), jnp.where(first, left, right)


def sweep_kernel(
    source_plane,
    rate_low,
    rate_own,
    rate_high,
    state_low,
    state_own,
    state_high,
    velocity_ref,
    profile_ref,
    count1,
    count2,
    sum1,
    sum2,
    columns_table,
    out_ref,
    half_rate,
    state0,
    state1,
    adjoint2,
    adjoint1,
    face_x,
    grad_x0,
    grad_x1,
    grad_x2,
    inject1,
    depth_product,
    pair_sum,
    coarse_rows,
):
    index = pl.program_id(0)
    total = pl.num_programs(0)
    size = half_rate.shape[2] - 2 * PAD
    halves = range(2)
    strips = range(0, size, STRIP)

    def rows(ref, plane, half, start, shift=0):
        slot = plane & (ref.shape[0] - 1)
        return ref[slot, half, PAD + start + shift : PAD + start + shift + STRIP, :]

    def put(ref, plane, half, start, value):
        slot = plane & (ref.shape[0] - 1)
        ref[slot, half, PAD + start : PAD + start + STRIP, :] = value
        if start == 0:
            ref[slot, half, PAD + size : PAD + size + 1, :] = value[:1]
        if start + STRIP == size:
            ref[slot, half, PAD - 1 : PAD, :] = value[STRIP - 1 :]

    def plain(ref, plane, half, start):
        return ref[plane & (ref.shape[0] - 1), half, start : start + STRIP, :]

    def put_plain(ref, plane, half, start, value):
        ref[plane & (ref.shape[0] - 1), half, start : start + STRIP, :] = value

    def enter(rate_ref, state_ref):
        for start in strips:
            span = slice(start, start + STRIP)
            rate, state = [], []
            for half in halves:
                cols = slice(half * LANES, (half + 1) * LANES)
                rate.append((0.5 * TIME_STEP) * jnp.exp(rate_ref[0, span, cols]))
                state.append(state_ref[0, span, cols])
            rate_ahead, state_ahead = ahead(rate), ahead(state)
            for half in halves:
                put(half_rate, index, half, start, rate[half])
                put(state0, index, half, start, state[half])
                put_plain(face_x, index, half, start, rate[half] + rate_ahead[half])
                put_plain(grad_x0, index, half, start, state_ahead[half] - state[half])

    @pl.when(index < HALO)
    def _():
        enter(rate_low, state_low)

    @pl.when((index >= HALO) & (index < total - HALO))
    def _():
        enter(rate_own, state_own)

    @pl.when((index >= total - HALO) & (index < total))
    def _():
        enter(rate_high, state_high)

    def advance(field, grad_x, slot, start, adjoint):
        up, down = slot + 1, slot - 1
        flux = [
            plain(face_x, slot, half, start) * plain(grad_x, slot, half, start) for half in halves
        ]
        flux_behind = behind(flux)
        result = []
        for half in halves:
            value = rows(field, slot, half, start)
            rate = rows(half_rate, slot, half, start)
            wind = TIME_STEP * velocity_ref[
                start : start + STRIP, half * LANES : (half + 1) * LANES
            ]
            rate_up = rate + rows(half_rate, up, half, start)
            rate_down = rate + rows(half_rate, down, half, start)
            if adjoint:
                rate_up = rate_up + wind
            else:
                rate_down = rate_down + wind
            depth_part = rate_up * (rows(field, up, half, start) - value) - rate_down * (
                value - rows(field, down, half, start)
            )
            row_part = (rate + rows(half_rate, slot, half, start, 1)) * (
                rows(field, slot, half, start, 1) - value
            ) - (rate + rows(half_rate, slot, half, start, -1)) * (
                value - rows(field, slot, half, start, -1)
            )
            result.append(value + depth_part + row_part + (flux[half] - flux_behind[half]))
        return result

    def save(field, grad_x, slot, start, parts):
        parts_ahead = ahead(parts)
        for half in halves:
            put(field, slot, half, start, parts[half])
            put_plain(grad_x, slot, half, start, parts_ahead[half] - parts[half])

    def source_gain(plane):
        return jnp.where(plane == source_plane[0], jnp.float32(TIME_STEP), jnp.float32(0.0))

    def source(gain, half, start):
        return gain * profile_ref[0, start : start + STRIP, half * LANES : (half + 1) * LANES]

    plane1 = index - 1

    @pl.when((plane1 >= 1) & (plane1 < total - 1))
    def _():
        slot = plane1
        gain = source_gain(plane1)
        for start in strips:
            parts = advance(state0, grad_x0, slot, start, False)
            parts = [parts[half] + source(gain, half, start) for half in halves]
            save(state1, grad_x1, slot, start, parts)

    plane2 = index - 2

    @pl.when((plane2 >= 2) & (plane2 < total - 2))
    def _():
        slot = plane2
        gain = source_gain(plane2)
        for start in strips:
            parts = advance(state1, grad_x1, slot, start, False)
            mu = []
            for half in halves:
                cols = slice(half * LANES, (half + 1) * LANES)
                state2 = parts[half] + source(gain, half, start)
                span = slice(start, start + STRIP)
                mu.append(count2[0, span, cols] * state2 - sum2[0, span, cols])
                put_plain(
                    inject1,
                    slot,
                    half,
                    start,
                    count1[0, span, cols] * rows(state1, slot, half, start) - sum1[0, span, cols],
                )
            save(adjoint2, grad_x2, slot, start, mu)

    plane3 = index - 3

    @pl.when((plane3 >= 3) & (plane3 < total - 3))
    def _():
        slot = plane3
        for start in strips:
            parts = advance(adjoint2, grad_x2, slot, start, True)
            for half in halves:
                put(
                    adjoint1,
                    slot,
                    half,
                    start,
                    parts[half] + plain(inject1, slot, half, start),
                )

    plane4 = index - 4

    def products(slot, other, half, start):
        def step(field):
            return rows(field, other, half, start) - rows(field, slot, half, start)

        return step(state0) * step(adjoint1) + step(state1) * step(adjoint2)

    @pl.when(plane4 == HALO - 1)
    def _():
        slot = plane4
        for start in strips:
            for half in halves:
                depth_product[half, start : start + STRIP, :] = products(
                    slot, slot + 1, half, start
                )

    @pl.when(plane4 >= HALO)
    def _():
        slot, up = plane4, plane4 + 1
        even = (plane4 & 1) == 0
        for start in strips:
            mu = [rows(adjoint1, slot, half, start) for half in halves]
            mu_ahead = ahead(mu)
            product_x = [
                plain(grad_x0, slot, half, start) * (mu_ahead[half] - mu[half])
                + plain(grad_x1, slot, half, start) * plain(grad_x2, slot, half, start)
                for half in halves
            ]
            product_behind = behind(product_x)
            for half in halves:
                span = slice(start, start + STRIP)
                result = product_x[half] + product_behind[half]
                upper = products(slot, up, half, start)
                result = result + (upper + depth_product[half, span, :])
                depth_product[half, span, :] = upper
                for shift in (1, -1):
                    factors = [
                        rows(field, slot, half, start, shift) - rows(field, slot, half, start)
                        for field in (state0, adjoint1, state1, adjoint2)
                    ]
                    result = result + (factors[0] * factors[1] + factors[2] * factors[3])
                result = -rows(half_rate, slot, half, start) * result
                pair_sum[half, span, :] = jnp.where(even, 0.0, pair_sum[half, span, :]) + result

    @pl.when((plane4 >= HALO) & ((plane4 & 1) == 1))
    def _():
        for half in halves:
            even_rows = pair_sum[half, pl.ds(0, size // R, R), :]
            odd_rows = pair_sum[half, pl.ds(1, size // R, R), :]
            cols = slice(half * LANES, (half + 1) * LANES)
            coarse_rows[(plane4 - HALO) >> 1, :, cols] = even_rows + odd_rows

    @pl.when(index == total - 1)
    def _():
        planes = coarse_rows.shape[0]
        for plane in range(planes):
            out_ref[pl.ds(plane, columns_table.shape[0], planes), :] = lax.dot_general(
                columns_table[...],
                coarse_rows[plane],
                (((1,), (1,)), ((), ())),
                precision=lax.Precision.HIGHEST,
                preferred_element_type=jnp.float32,
            )


def sweep(source_plane, rates, states, velocity, profile, fields):
    own, rows_count, cols_count = rates[1].shape
    total = own + 2 * HALO
    coarse = rows_count // R
    plane = (1, rows_count, cols_count)
    smem = pl.BlockSpec(memory_space=pltpu.SMEM)
    vmem = pl.BlockSpec(memory_space=pltpu.VMEM)
    low = pl.BlockSpec(plane, lambda i: (jnp.minimum(i, HALO - 1), 0, 0))
    middle = pl.BlockSpec(plane, lambda i: (jnp.clip(i - HALO, 0, own - 1), 0, 0))
    high = pl.BlockSpec(plane, lambda i: (jnp.clip(i - HALO - own, 0, HALO - 1), 0, 0))
    columns_table = jnp.asarray(np.repeat(hartley(cols_count // R), R, axis=1))
    voxels = pl.BlockSpec(
        (1, rows_count, cols_count),
        lambda i: (jnp.clip(i - HALO, 0, total - 2 * LEAD - 1), 0, 0),
    )
    def padded(kept):
        return pltpu.VMEM((kept, 2, rows_count + 2 * PAD, LANES), jnp.float32)

    def plain(kept):
        return pltpu.VMEM((kept, 2, rows_count, LANES), jnp.float32)

    return pl.pallas_call(
        sweep_kernel,
        grid=(total,),
        out_shape=jax.ShapeDtypeStruct((cols_count // R * (own // R), coarse), jnp.float32),
        in_specs=[smem, low, middle, high, low, middle, high, vmem, vmem] + [voxels] * 4 + [vmem],
        out_specs=vmem,
        scratch_shapes=[padded(LONG)] * 2
        + [padded(SHORT)] * 3
        + [plain(SHORT), plain(LONG), plain(SHORT), plain(SHORT), plain(2)]
        + [
            pltpu.VMEM((2, rows_count, LANES), jnp.float32),
            pltpu.VMEM((2, rows_count, LANES), jnp.float32),
            pltpu.VMEM((own // R, coarse, cols_count), jnp.float32),
        ],
        compiler_params=pltpu.CompilerParams(
            vmem_limit_bytes=19 * 2**20, dimension_semantics=("arbitrary",)
        ),
        cost_estimate=pl.CostEstimate(
            flops=200_000_000, bytes_accessed=34 * 2**20, transcendentals=0
        ),
        name="sweep",
    )(
        source_plane,
        *rates,
        *states,
        velocity,
        profile,
        *fields,
        columns_table,
    )


def exact_dot(a, b):
    return jnp.dot(a, b, precision=lax.Precision.HIGHEST, preferred_element_type=jnp.float32)


def filter_kernel(lam_second, received, table_ref, symbol_depth, symbol_rows, out_ref, field):
    depth_blocks, tracers, planes, size = received.shape
    for block in range(depth_blocks):
        field[block * planes : (block + 1) * planes, :] = jnp.sum(received[block], axis=0)
    table = table_ref[...]
    spectrum = exact_dot(exact_dot(table, field[...]), table)
    lam = symbol_depth[...] + symbol_rows[...] + lam_second[0]
    factor = 1.0 + PRIOR_RANGE * lam
    spectrum = spectrum * (1.0 / (factor * factor) / float(size**3))
    field[...] = exact_dot(exact_dot(table, spectrum), table)
    share = size // tracers
    group = lax.broadcasted_iota(jnp.int32, (depth_blocks, size), 1) // share
    by_plane = [field[pl.ds(plane, depth_blocks, planes), :] for plane in range(planes)]
    for tracer in range(tracers):
        part = jnp.zeros((depth_blocks, size), jnp.float32)
        for plane in range(planes):
            shift = (plane - tracer) * share % size
            moved = pltpu.roll(by_plane[plane], shift, 1) if shift else by_plane[plane]
            part = jnp.where(group == plane, moved, part)
        out_ref[pl.ds(tracer, depth_blocks, tracers), :] = part


def filtered(received, own_symbol):
    depth_blocks, tracers, planes, size = received.shape
    line = symbol(size)
    vmem = pl.BlockSpec(memory_space=pltpu.VMEM)
    return pl.pallas_call(
        filter_kernel,
        out_shape=jax.ShapeDtypeStruct((depth_blocks * tracers, size), jnp.float32),
        in_specs=[pl.BlockSpec(memory_space=pltpu.SMEM)] + [vmem] * 4,
        out_specs=vmem,
        scratch_shapes=[pltpu.VMEM((depth_blocks * planes, size), jnp.float32)],
        compiler_params=pltpu.CompilerParams(vmem_limit_bytes=16 * 2**20),
        name="filter",
    )(
        own_symbol,
        received,
        jnp.asarray(hartley(size)),
        jnp.asarray(line[:, None]),
        jnp.asarray(line[None, :]),
    )


def inverse_kernel(received, table_ref, out_ref):
    out_ref[...] = lax.dot_general(
        received[...],
        table_ref[...],
        (((0,), (0,)), ((), ())),
        precision=lax.Precision.HIGHEST,
        preferred_element_type=jnp.float32,
    )


def inverse_columns(received):
    vmem = pl.BlockSpec(memory_space=pltpu.VMEM)
    return pl.pallas_call(
        inverse_kernel,
        out_shape=jax.ShapeDtypeStruct(received.shape, jnp.float32),
        in_specs=[vmem, vmem],
        out_specs=vmem,
        compiler_params=pltpu.CompilerParams(vmem_limit_bytes=16 * 2**20),
        name="inverse_columns",
    )(received, jnp.asarray(hartley(received.shape[0])))


def neighbours(array):
    count = lax.axis_size("domain")
    up = [(i, (i + 1) % count) for i in range(count)]
    down = [(j, i) for i, j in up]
    before = lax.ppermute(array[-HALO:], "domain", up)
    after = lax.ppermute(array[:HALO], "domain", down)
    return before, array, after


def local(log_rate, velocity, initial, profile, plane, depth, row, column, step_of, observed):
    slab, rows_count, cols_count = log_rate.shape
    domain_count, tracer_count = lax.axis_size("domain"), lax.axis_size("tracer")
    full = slab * domain_count
    offset = lax.axis_index("domain") * slab
    rates = neighbours(log_rate)
    states = neighbours(initial[0])
    keys, values, starts = sort_probes(
        offset.astype(jnp.int32)[None],
        depth,
        row,
        column,
        step_of,
        observed,
        slab + 2 * LEAD,
    )
    source_plane = (plane - (offset - HALO)) % full
    fields = bin_probes(starts, keys, values, rows_count, cols_count)
    spectral = sweep(source_plane, rates, states, velocity, profile, fields)
    first, planes, second = rows_count // R, slab // R, cols_count // R
    axes = ("domain", "tracer")
    received = lax.all_to_all(
        spectral.reshape(second, planes, first), axes, split_axis=0, concat_axis=0, tiled=True
    )
    own = lax.axis_index("domain") * tracer_count + lax.axis_index("tracer")
    own_symbol = lax.dynamic_slice(jnp.asarray(symbol(second)), (own,), (1,))
    back = filtered(received.reshape(domain_count, tracer_count, planes, first), own_symbol)
    result = lax.all_to_all(back, axes, split_axis=0, concat_axis=0, tiled=True)
    return inverse_columns(result).reshape(planes, first // tracer_count, second)


def solution(mesh):
    return jax.shard_map(
        local,
        mesh=mesh,
        in_specs=(
            P("domain", None, None),
            P(),
            P("tracer", "domain", None, None),
            P("tracer", None, None),
            P("tracer"),
            P("tracer", None),
            P("tracer", None),
            P("tracer", None),
            P("tracer", None),
            P("tracer", None),
        ),
        out_specs=P("domain", "tracer", None),
        check_vma=False,
    )
```

```python
import functools
import math

import jax
import jax.numpy as jnp
import numpy as np
from jax import lax
from jax.experimental import pallas as pl
from jax.experimental.pallas import tpu as pltpu
from jax.sharding import PartitionSpec as P

R = 2
STEPS = 2
TIME_STEP = 0.14
PRIOR_RANGE = 4.0

HALO = 4
LEAD = 2
LANES = 128
LONG, SHORT = 8, 4
PAD = 8
STRIP = 32


def hartley(length):
    phases = np.outer(np.arange(length), np.arange(length)) % length
    angles = 2.0 * math.pi / length * phases
    return (np.cos(angles) + np.sin(angles)).astype(np.float32)


def symbol(length):
    return (2.0 - 2.0 * np.cos(2.0 * math.pi / length * np.arange(length))).astype(np.float32)


def sort_kernel(
    offset_ref,
    depth_ref,
    row_ref,
    column_ref,
    step_ref,
    observed_ref,
    rate,
    state,
    keys_out,
    values_out,
    starts_out,
    rate_near,
    state_near,
    keys,
    values,
    sems,
):
    near = [
        pltpu.make_async_copy(rate, rate_near, sems.at[0]),
        pltpu.make_async_copy(state, state_near, sems.at[1]),
    ]
    for copy in near:
        copy.start()
    offset = offset_ref[0]
    plane = (depth_ref[...] - (offset - LEAD)) & 255
    key = (plane << 17) | ((step_ref[...] - 1) << 16) | (row_ref[...] << 8) | column_ref[...]
    keys[...] = key.reshape(keys.shape)
    values[...] = observed_ref[...].reshape(values.shape)
    for index in range(starts_out.shape[0]):
        if index == 0:
            starts_out[index] = 0
        else:
            starts_out[index] = jnp.sum((key < (index << 17)).astype(jnp.int32))

    lane = lax.broadcasted_iota(jnp.int32, (8, LANES), 1)
    sublane = lax.broadcasted_iota(jnp.int32, (8, LANES), 0)

    def pair(low, high, down):
        (key_a, value_a), (key_b, value_b) = low, high
        if down is False:
            swap = key_a > key_b
        elif down is True:
            swap = key_a < key_b
        else:
            swap = jnp.logical_xor(key_a > key_b, down)
        return (
            (jnp.where(swap, key_b, key_a), jnp.where(swap, value_b, value_a)),
            (jnp.where(swap, key_a, key_b), jnp.where(swap, value_a, value_b)),
        )

    def within(item, axis, distance, upper, largest):
        key, value = item
        size = key.shape[axis]
        key_p = jnp.where(
            upper, pltpu.roll(key, distance, axis), pltpu.roll(key, size - distance, axis)
        )
        value_p = jnp.where(
            upper, pltpu.roll(value, distance, axis), pltpu.roll(value, size - distance, axis)
        )
        gap = key_p - key
        take = jnp.where(largest, gap, -gap) > 0
        return jnp.where(take, key_p, key), jnp.where(take, value_p, value)

    def bit_of(array, bit):
        return ((array >> bit) & 1) == 1

    def registers(items, level, down):
        for bit in range(level, -1, -1):
            for low in range(16):
                if low & (1 << bit):
                    continue
                high = low | (1 << bit)
                order = down(low) if callable(down) else down
                items[low], items[high] = pair(items[low], items[high], order)
        return items

    def sublanes(items, bit, down):
        upper = bit_of(sublane, bit)
        largest = jnp.logical_xor(upper, down) if not isinstance(down, bool) else (
            jnp.logical_not(upper) if down else upper
        )
        return [within(item, 0, 1 << bit, upper, largest) for item in items]

    def load(group):
        return [(keys[group * 16 + i], values[group * 16 + i]) for i in range(16)]

    def store(group, items):
        for i, (key, value) in enumerate(items):
            keys[group * 16 + i] = key
            values[group * 16 + i] = value

    for group in range(2):
        items = load(group)
        for level in range(1, 4):
            items = registers(
                items, level - 1, lambda low, level=level: bool((low >> level) & 1)
            )
        items = registers(items, 3, bit_of(sublane, 0))
        for level in range(1, 3):
            down = bit_of(sublane, level)
            for bit in range(level - 1, -1, -1):
                items = sublanes(items, bit, down)
            items = registers(items, 3, down)
        down = bool(group)
        for bit in range(2, -1, -1):
            items = sublanes(items, bit, down)
        items = registers(items, 3, down)
        store(group, items)

    def merge(level, carry):
        down = ((lane >> level) & 1) == 1

        def across(turn, inner):
            bit = level - 1 - turn
            distance = jnp.int32(1) << bit
            upper = ((lane >> bit) & 1) == 1
            largest = jnp.logical_xor(upper, down)
            for i in range(32):
                keys[i], values[i] = within((keys[i], values[i]), 1, distance, upper, largest)
            return inner

        lax.fori_loop(0, level, across, 0)
        for i in range(16):
            low, high = pair((keys[i], values[i]), (keys[i + 16], values[i + 16]), down)
            keys[i], values[i] = low
            keys[i + 16], values[i + 16] = high
        for group in range(2):
            items = load(group)
            for bit in range(2, -1, -1):
                items = sublanes(items, bit, down)
            items = registers(items, 3, down)
            store(group, items)
        return carry

    lax.fori_loop(0, 8, merge, 0)

    for half in range(2):
        part = keys[pl.ds(half * 16, 16)].reshape(LANES, LANES)
        keys_out[pl.ds(half, LANES, 2), :] = part.T
        part = values[pl.ds(half * 16, 16)].reshape(LANES, LANES)
        values_out[pl.ds(half, LANES, 2), :] = part.T
    keys_out[2 * LANES :, :] = jnp.full((8, LANES), -1, jnp.int32)
    values_out[2 * LANES :, :] = jnp.zeros((8, LANES), jnp.float32)
    for copy in near:
        copy.wait()


def sort_probes(offset, depth, row, column, step_of, observed, planes, rate, state):
    count = depth.size
    shape = (count // LANES, LANES)
    vmem = pl.BlockSpec(memory_space=pltpu.VMEM)
    smem = pl.BlockSpec(memory_space=pltpu.SMEM)
    stay = pl.BlockSpec(memory_space=pl.ANY)
    return pl.pallas_call(
        sort_kernel,
        out_shape=(
            jax.ShapeDtypeStruct((shape[0] + 8, LANES), jnp.int32),
            jax.ShapeDtypeStruct((shape[0] + 8, LANES), jnp.float32),
            jax.ShapeDtypeStruct((planes + 1,), jnp.int32),
            jax.ShapeDtypeStruct(rate.shape, jnp.float32),
            jax.ShapeDtypeStruct(state.shape, jnp.float32),
        ),
        in_specs=[smem] + [vmem] * 5 + [stay] * 2,
        out_specs=(vmem, vmem, smem, stay, stay),
        scratch_shapes=[
            pltpu.VMEM((shape[0] // 8, 8, LANES), jnp.int32),
            pltpu.VMEM((shape[0] // 8, 8, LANES), jnp.float32),
            pltpu.SemaphoreType.DMA((2,)),
        ],
        compiler_params=pltpu.CompilerParams(vmem_limit_bytes=42 * 2**20),
        cost_estimate=pl.CostEstimate(flops=20_000_000, bytes_accessed=2**20, transcendentals=0),
        name="sort_probes",
    )(offset, *(a.reshape(shape) for a in (depth, row, column, step_of, observed)), rate, state)


def bin_kernel(starts, keys_ref, values_ref, *fields):
    place = pl.program_id(0)
    size = fields[0].shape[1]
    both = STEPS * size
    counts, sums = fields[:STEPS], fields[STEPS:]
    begin, end = starts[place], starts[place + 1]
    first = begin >> 7
    windows = (end - (first << 7) + 2 * LANES - 1) >> 8

    def window(turn):
        at = first + 2 * turn
        key = jnp.concatenate([keys_ref[pl.ds(at, 1), :], keys_ref[pl.ds(at + 1, 1), :]], axis=1)
        value = jnp.concatenate(
            [values_ref[pl.ds(at, 1), :], values_ref[pl.ds(at + 1, 1), :]], axis=1
        )
        target = lax.broadcasted_iota(jnp.int32, (both, 2 * LANES), 0) + (place << 9)
        in_row = jnp.where((key >> 8) == target, 1.0, 0.0).astype(jnp.bfloat16)
        in_column = (key & 255) == lax.broadcasted_iota(jnp.int32, (size, 2 * LANES), 0)
        coarse = value.astype(jnp.bfloat16).astype(jnp.float32)
        rest = value - coarse

        def product(amount):
            return lax.dot_general(
                in_row,
                jnp.where(in_column, amount, 0.0).astype(jnp.bfloat16),
                (((1,), (1,)), ((), ())),
                preferred_element_type=jnp.float32,
            )

        return product(1.0), product(coarse) + product(rest)

    def parts(pair):
        for fields_of, values in zip((counts, sums), pair):
            for step, field in enumerate(fields_of):
                yield field, values[step * size : (step + 1) * size]

    for field, value in parts(window(0)):
        field[0] = value

    def more(turn, carry):
        for field, value in parts(window(turn)):
            field[0] += value
        return carry

    lax.fori_loop(1, windows, more, 0)


def bin_probes(starts, keys, values, rows_count, cols_count):
    places = starts.shape[0] - 1
    vmem = pl.BlockSpec(memory_space=pltpu.VMEM)
    block = pl.BlockSpec((1, rows_count, cols_count), lambda i: (i, 0, 0))
    field = jax.ShapeDtypeStruct((places, rows_count, cols_count), jnp.float32)
    return pl.pallas_call(
        bin_kernel,
        grid=(places,),
        out_shape=(field,) * (2 * STEPS),
        in_specs=[pl.BlockSpec(memory_space=pltpu.SMEM), vmem, vmem],
        out_specs=(block,) * (2 * STEPS),
        compiler_params=pltpu.CompilerParams(
            vmem_limit_bytes=5 * 2**20, dimension_semantics=("arbitrary",)
        ),
        cost_estimate=pl.CostEstimate(
            flops=30_000_000, bytes_accessed=20 * 2**20, transcendentals=0
        ),
        name="bin_probes",
    )(starts, keys, values)


def ahead(parts):
    lane = lax.broadcasted_iota(jnp.int32, parts[0].shape, 1)
    left, right = (pltpu.roll(part, LANES - 1, 1) for part in parts)
    last = lane == LANES - 1
    return jnp.where(last, right, left), jnp.where(last, left, right)


def behind(parts):
    lane = lax.broadcasted_iota(jnp.int32, parts[0].shape, 1)
    left, right = (pltpu.roll(part, 1, 1) for part in parts)
    first = lane == 0
    return jnp.where(first, right, left), jnp.where(first, left, right)


def sweep_kernel(
    source_plane,
    rate_low,
    rate_own,
    rate_high,
    state_low,
    state_own,
    state_high,
    velocity_ref,
    profile_ref,
    count1,
    count2,
    sum1,
    sum2,
    columns_table,
    out_ref,
    half_rate,
    state0,
    state1,
    adjoint2,
    adjoint1,
    face_x,
    grad_x0,
    grad_x1,
    grad_x2,
    inject1,
    depth_product,
    pair_sum,
    coarse_rows,
):
    index = pl.program_id(0)
    total = pl.num_programs(0)
    size = half_rate.shape[2] - 2 * PAD
    halves = range(2)
    strips = range(0, size, STRIP)

    def rows(ref, plane, half, start, shift=0):
        slot = plane & (ref.shape[0] - 1)
        return ref[slot, half, PAD + start + shift : PAD + start + shift + STRIP, :]

    def put(ref, plane, half, start, value):
        slot = plane & (ref.shape[0] - 1)
        ref[slot, half, PAD + start : PAD + start + STRIP, :] = value
        if start == 0:
            ref[slot, half, PAD + size : PAD + size + 1, :] = value[:1]
        if start + STRIP == size:
            ref[slot, half, PAD - 1 : PAD, :] = value[STRIP - 1 :]

    def plain(ref, plane, half, start):
        return ref[plane & (ref.shape[0] - 1), half, start : start + STRIP, :]

    def put_plain(ref, plane, half, start, value):
        ref[plane & (ref.shape[0] - 1), half, start : start + STRIP, :] = value

    def enter(rate_ref, state_ref):
        for start in strips:
            span = slice(start, start + STRIP)
            rate, state = [], []
            for half in halves:
                cols = slice(half * LANES, (half + 1) * LANES)
                rate.append((0.5 * TIME_STEP) * jnp.exp(rate_ref[0, span, cols]))
                state.append(state_ref[0, span, cols])
            rate_ahead, state_ahead = ahead(rate), ahead(state)
            for half in halves:
                put(half_rate, index, half, start, rate[half])
                put(state0, index, half, start, state[half])
                put_plain(face_x, index, half, start, rate[half] + rate_ahead[half])
                put_plain(grad_x0, index, half, start, state_ahead[half] - state[half])

    @pl.when(index < HALO)
    def _():
        enter(rate_low, state_low)

    @pl.when((index >= HALO) & (index < total - HALO))
    def _():
        enter(rate_own, state_own)

    @pl.when((index >= total - HALO) & (index < total))
    def _():
        enter(rate_high, state_high)

    def advance(field, grad_x, slot, start, adjoint):
        up, down = slot + 1, slot - 1
        flux = [
            plain(face_x, slot, half, start) * plain(grad_x, slot, half, start) for half in halves
        ]
        flux_behind = behind(flux)
        result = []
        for half in halves:
            value = rows(field, slot, half, start)
            rate = rows(half_rate, slot, half, start)
            wind = TIME_STEP * velocity_ref[
                start : start + STRIP, half * LANES : (half + 1) * LANES
            ]
            rate_up = rate + rows(half_rate, up, half, start)
            rate_down = rate + rows(half_rate, down, half, start)
            if adjoint:
                rate_up = rate_up + wind
            else:
                rate_down = rate_down + wind
            depth_part = rate_up * (rows(field, up, half, start) - value) - rate_down * (
                value - rows(field, down, half, start)
            )
            row_part = (rate + rows(half_rate, slot, half, start, 1)) * (
                rows(field, slot, half, start, 1) - value
            ) - (rate + rows(half_rate, slot, half, start, -1)) * (
                value - rows(field, slot, half, start, -1)
            )
            result.append(value + depth_part + row_part + (flux[half] - flux_behind[half]))
        return result

    def save(field, grad_x, slot, start, parts):
        parts_ahead = ahead(parts)
        for half in halves:
            put(field, slot, half, start, parts[half])
            put_plain(grad_x, slot, half, start, parts_ahead[half] - parts[half])

    def source_gain(plane):
        return jnp.where(plane == source_plane[0], jnp.float32(TIME_STEP), jnp.float32(0.0))

    def source(gain, half, start):
        return gain * profile_ref[0, start : start + STRIP, half * LANES : (half + 1) * LANES]

    plane1 = index - 1

    @pl.when((plane1 >= 1) & (plane1 < total - 1))
    def _():
        slot = plane1
        gain = source_gain(plane1)
        for start in strips:
            parts = advance(state0, grad_x0, slot, start, False)
            parts = [parts[half] + source(gain, half, start) for half in halves]
            save(state1, grad_x1, slot, start, parts)

    plane2 = index - 2

    @pl.when((plane2 >= 2) & (plane2 < total - 2))
    def _():
        slot = plane2
        gain = source_gain(plane2)
        for start in strips:
            parts = advance(state1, grad_x1, slot, start, False)
            mu = []
            for half in halves:
                cols = slice(half * LANES, (half + 1) * LANES)
                state2 = parts[half] + source(gain, half, start)
                span = slice(start, start + STRIP)
                mu.append(count2[0, span, cols] * state2 - sum2[0, span, cols])
                put_plain(
                    inject1,
                    slot,
                    half,
                    start,
                    count1[0, span, cols] * rows(state1, slot, half, start) - sum1[0, span, cols],
                )
            save(adjoint2, grad_x2, slot, start, mu)

    plane3 = index - 3

    @pl.when((plane3 >= 3) & (plane3 < total - 3))
    def _():
        slot = plane3
        for start in strips:
            parts = advance(adjoint2, grad_x2, slot, start, True)
            for half in halves:
                put(
                    adjoint1,
                    slot,
                    half,
                    start,
                    parts[half] + plain(inject1, slot, half, start),
                )

    plane4 = index - 4

    def products(slot, other, half, start):
        def step(field):
            return rows(field, other, half, start) - rows(field, slot, half, start)

        return step(state0) * step(adjoint1) + step(state1) * step(adjoint2)

    @pl.when(plane4 == HALO - 1)
    def _():
        slot = plane4
        for start in strips:
            for half in halves:
                depth_product[half, start : start + STRIP, :] = products(
                    slot, slot + 1, half, start
                )

    @pl.when(plane4 >= HALO)
    def _():
        slot, up = plane4, plane4 + 1
        even = (plane4 & 1) == 0
        for start in strips:
            mu = [rows(adjoint1, slot, half, start) for half in halves]
            mu_ahead = ahead(mu)
            product_x = [
                plain(grad_x0, slot, half, start) * (mu_ahead[half] - mu[half])
                + plain(grad_x1, slot, half, start) * plain(grad_x2, slot, half, start)
                for half in halves
            ]
            product_behind = behind(product_x)
            for half in halves:
                span = slice(start, start + STRIP)
                result = product_x[half] + product_behind[half]
                upper = products(slot, up, half, start)
                result = result + (upper + depth_product[half, span, :])
                depth_product[half, span, :] = upper
                for shift in (1, -1):
                    factors = [
                        rows(field, slot, half, start, shift) - rows(field, slot, half, start)
                        for field in (state0, adjoint1, state1, adjoint2)
                    ]
                    result = result + (factors[0] * factors[1] + factors[2] * factors[3])
                result = -rows(half_rate, slot, half, start) * result
                pair_sum[half, span, :] = jnp.where(even, 0.0, pair_sum[half, span, :]) + result

    @pl.when((plane4 >= HALO) & ((plane4 & 1) == 1))
    def _():
        for half in halves:
            even_rows = pair_sum[half, pl.ds(0, size // R, R), :]
            odd_rows = pair_sum[half, pl.ds(1, size // R, R), :]
            cols = slice(half * LANES, (half + 1) * LANES)
            coarse_rows[(plane4 - HALO) >> 1, :, cols] = even_rows + odd_rows

    @pl.when(index == total - 1)
    def _():
        planes = coarse_rows.shape[0]
        for plane in range(planes):
            out_ref[pl.ds(plane, columns_table.shape[0], planes), :] = lax.dot_general(
                columns_table[...],
                coarse_rows[plane],
                (((1,), (1,)), ((), ())),
                precision=lax.Precision.HIGHEST,
                preferred_element_type=jnp.float32,
            )


def sweep(source_plane, rates, states, velocity, profile, fields):
    own, rows_count, cols_count = rates[1].shape
    total = own + 2 * HALO
    coarse = rows_count // R
    plane = (1, rows_count, cols_count)
    smem = pl.BlockSpec(memory_space=pltpu.SMEM)
    vmem = pl.BlockSpec(memory_space=pltpu.VMEM)
    low = pl.BlockSpec(plane, lambda i: (jnp.minimum(i, HALO - 1), 0, 0))
    middle = pl.BlockSpec(plane, lambda i: (jnp.clip(i - HALO, 0, own - 1), 0, 0))
    high = pl.BlockSpec(plane, lambda i: (jnp.clip(i - HALO - own, 0, HALO - 1), 0, 0))
    columns_table = jnp.asarray(np.repeat(hartley(cols_count // R), R, axis=1))
    voxels = pl.BlockSpec(
        (1, rows_count, cols_count),
        lambda i: (jnp.clip(i - HALO, 0, total - 2 * LEAD - 1), 0, 0),
    )
    def padded(kept):
        return pltpu.VMEM((kept, 2, rows_count + 2 * PAD, LANES), jnp.float32)

    def plain(kept):
        return pltpu.VMEM((kept, 2, rows_count, LANES), jnp.float32)

    return pl.pallas_call(
        sweep_kernel,
        grid=(total,),
        out_shape=jax.ShapeDtypeStruct((cols_count // R * (own // R), coarse), jnp.float32),
        in_specs=[smem, low, middle, high, low, middle, high, vmem, vmem] + [voxels] * 4 + [vmem],
        out_specs=vmem,
        scratch_shapes=[padded(LONG)] * 2
        + [padded(SHORT)] * 3
        + [plain(SHORT), plain(LONG), plain(SHORT), plain(SHORT), plain(2)]
        + [
            pltpu.VMEM((2, rows_count, LANES), jnp.float32),
            pltpu.VMEM((2, rows_count, LANES), jnp.float32),
            pltpu.VMEM((own // R, coarse, cols_count), jnp.float32),
        ],
        compiler_params=pltpu.CompilerParams(
            vmem_limit_bytes=18 * 2**20, dimension_semantics=("arbitrary",)
        ),
        cost_estimate=pl.CostEstimate(
            flops=200_000_000, bytes_accessed=34 * 2**20, transcendentals=0
        ),
        name="sweep",
    )(
        source_plane,
        *rates,
        *states,
        velocity,
        profile,
        *fields,
        columns_table,
    )


def exact_dot(a, b):
    return jnp.dot(a, b, precision=lax.Precision.HIGHEST, preferred_element_type=jnp.float32)


def filter_kernel(lam_second, received, table_ref, symbol_depth, symbol_rows, out_ref, field):
    depth_blocks, tracers, planes, size = received.shape
    for block in range(depth_blocks):
        field[block * planes : (block + 1) * planes, :] = jnp.sum(received[block], axis=0)
    table = table_ref[...]
    spectrum = exact_dot(exact_dot(table, field[...]), table)
    lam = symbol_depth[...] + symbol_rows[...] + lam_second[0]
    factor = 1.0 + PRIOR_RANGE * lam
    spectrum = spectrum * (1.0 / (factor * factor) / float(size**3))
    field[...] = exact_dot(exact_dot(table, spectrum), table)
    share = size // tracers
    group = lax.broadcasted_iota(jnp.int32, (depth_blocks, size), 1) // share
    by_plane = [field[pl.ds(plane, depth_blocks, planes), :] for plane in range(planes)]
    for tracer in range(tracers):
        part = jnp.zeros((depth_blocks, size), jnp.float32)
        for plane in range(planes):
            shift = (plane - tracer) * share % size
            moved = pltpu.roll(by_plane[plane], shift, 1) if shift else by_plane[plane]
            part = jnp.where(group == plane, moved, part)
        out_ref[pl.ds(tracer, depth_blocks, tracers), :] = part


def filtered(received, own_symbol):
    depth_blocks, tracers, planes, size = received.shape
    line = symbol(size)
    vmem = pl.BlockSpec(memory_space=pltpu.VMEM)
    return pl.pallas_call(
        filter_kernel,
        out_shape=jax.ShapeDtypeStruct((depth_blocks * tracers, size), jnp.float32),
        in_specs=[pl.BlockSpec(memory_space=pltpu.SMEM)] + [vmem] * 4,
        out_specs=vmem,
        scratch_shapes=[pltpu.VMEM((depth_blocks * planes, size), jnp.float32)],
        compiler_params=pltpu.CompilerParams(vmem_limit_bytes=16 * 2**20),
        name="filter",
    )(
        own_symbol,
        received,
        jnp.asarray(hartley(size)),
        jnp.asarray(line[:, None]),
        jnp.asarray(line[None, :]),
    )


def inverse_kernel(received, table_ref, out_ref):
    out_ref[...] = lax.dot_general(
        received[...],
        table_ref[...],
        (((0,), (0,)), ((), ())),
        precision=lax.Precision.HIGHEST,
        preferred_element_type=jnp.float32,
    )


def inverse_columns(received):
    vmem = pl.BlockSpec(memory_space=pltpu.VMEM)
    return pl.pallas_call(
        inverse_kernel,
        out_shape=jax.ShapeDtypeStruct(received.shape, jnp.float32),
        in_specs=[vmem, vmem],
        out_specs=vmem,
        compiler_params=pltpu.CompilerParams(vmem_limit_bytes=16 * 2**20),
        name="inverse_columns",
    )(received, jnp.asarray(hartley(received.shape[0])))


def edges_kernel(rate, state, rate_first, rate_last, state_first, state_last, sems):
    last = rate.shape[0] - HALO
    copies = [
        pltpu.make_async_copy(source.at[pl.ds(begin, HALO)], target, sems.at[at])
        for at, (source, begin, target) in enumerate(
            (
                (rate, last, rate_last),
                (rate, 0, rate_first),
                (state, last, state_last),
                (state, 0, state_first),
            )
        )
    ]
    for copy in copies:
        copy.start()
    for copy in copies:
        copy.wait()


def edges(rate, state):
    stay = pl.BlockSpec(memory_space=pl.ANY)
    end = jax.ShapeDtypeStruct((HALO, *rate.shape[1:]), jnp.float32)
    return pl.pallas_call(
        edges_kernel,
        out_shape=(end,) * 4,
        in_specs=[stay] * 2,
        out_specs=(stay,) * 4,
        scratch_shapes=[pltpu.SemaphoreType.DMA((4,))],
        compiler_params=pltpu.CompilerParams(vmem_limit_bytes=60 * 2**20),
        name="edges",
    )(rate, state)


def neighbours(first, last):
    count = lax.axis_size("domain")
    up = [(i, (i + 1) % count) for i in range(count)]
    down = [(j, i) for i, j in up]
    return lax.ppermute(last, "domain", up), lax.ppermute(first, "domain", down)


def local(log_rate, velocity, initial, profile, plane, depth, row, column, step_of, observed):
    slab, rows_count, cols_count = log_rate.shape
    domain_count, tracer_count = lax.axis_size("domain"), lax.axis_size("tracer")
    full = slab * domain_count
    offset = lax.axis_index("domain") * slab
    rate_first, rate_last, state_first, state_last = edges(log_rate, initial[0])
    rate_low, rate_high = neighbours(rate_first, rate_last)
    state_low, state_high = neighbours(state_first, state_last)
    keys, values, starts, rate_near, state_near = sort_probes(
        offset.astype(jnp.int32)[None],
        depth,
        row,
        column,
        step_of,
        observed,
        slab + 2 * LEAD,
        log_rate,
        initial[0],
    )
    source_plane = (plane - (offset - HALO)) % full
    fields = bin_probes(starts, keys, values, rows_count, cols_count)
    rates = (rate_low, rate_near, rate_high)
    states = (state_low, state_near, state_high)
    spectral = sweep(source_plane, rates, states, velocity, profile, fields)
    first, planes, second = rows_count // R, slab // R, cols_count // R
    axes = ("domain", "tracer")
    received = lax.all_to_all(
        spectral.reshape(second, planes, first), axes, split_axis=0, concat_axis=0, tiled=True
    )
    own = lax.axis_index("domain") * tracer_count + lax.axis_index("tracer")
    own_symbol = lax.dynamic_slice(jnp.asarray(symbol(second)), (own,), (1,))
    back = filtered(received.reshape(domain_count, tracer_count, planes, first), own_symbol)
    result = lax.all_to_all(back, axes, split_axis=0, concat_axis=0, tiled=True)
    return inverse_columns(result).reshape(planes, first // tracer_count, second)


def solution(mesh):
    return jax.shard_map(
        local,
        mesh=mesh,
        in_specs=(
            P("domain", None, None),
            P(),
            P("tracer", "domain", None, None),
            P("tracer", None, None),
            P("tracer"),
            P("tracer", None),
            P("tracer", None),
            P("tracer", None),
            P("tracer", None),
            P("tracer", None),
        ),
        out_specs=P("domain", "tracer", None),
        check_vma=False,
    )
```

```python
import functools
import math

import jax
import jax.numpy as jnp
import numpy as np
from jax import lax
from jax.experimental import pallas as pl
from jax.experimental.pallas import tpu as pltpu
from jax.sharding import PartitionSpec as P

R = 2
STEPS = 2
TIME_STEP = 0.14
PRIOR_RANGE = 4.0

HALO = 4
LEAD = 2
LANES = 128
LONG, SHORT = 8, 4
PAD = 8
STRIP = 32


def hartley(length):
    phases = np.outer(np.arange(length), np.arange(length)) % length
    angles = 2.0 * math.pi / length * phases
    return (np.cos(angles) + np.sin(angles)).astype(np.float32)


def symbol(length):
    return (2.0 - 2.0 * np.cos(2.0 * math.pi / length * np.arange(length))).astype(np.float32)


def sort_kernel(
    offset_ref,
    depth_ref,
    row_ref,
    column_ref,
    step_ref,
    observed_ref,
    rate,
    state,
    keys_out,
    values_out,
    starts_out,
    rate_near,
    state_near,
    keys,
    values,
    sems,
):
    near = [
        pltpu.make_async_copy(rate, rate_near, sems.at[0]),
        pltpu.make_async_copy(state, state_near, sems.at[1]),
    ]
    for copy in near:
        copy.start()
    offset = offset_ref[0]
    plane = (depth_ref[...] - (offset - LEAD)) & 255
    key = (plane << 17) | ((step_ref[...] - 1) << 16) | (row_ref[...] << 8) | column_ref[...]
    keys[...] = key.reshape(keys.shape)
    values[...] = observed_ref[...].reshape(values.shape)
    for index in range(starts_out.shape[0]):
        if index == 0:
            starts_out[index] = 0
        else:
            starts_out[index] = jnp.sum((key < (index << 17)).astype(jnp.int32))

    lane = lax.broadcasted_iota(jnp.int32, (8, LANES), 1)
    sublane = lax.broadcasted_iota(jnp.int32, (8, LANES), 0)

    def pair(low, high, down):
        (key_a, value_a), (key_b, value_b) = low, high
        if down is False:
            swap = key_a > key_b
        elif down is True:
            swap = key_a < key_b
        else:
            swap = jnp.logical_xor(key_a > key_b, down)
        return (
            (jnp.where(swap, key_b, key_a), jnp.where(swap, value_b, value_a)),
            (jnp.where(swap, key_a, key_b), jnp.where(swap, value_a, value_b)),
        )

    def within(item, axis, distance, upper, largest):
        key, value = item
        size = key.shape[axis]
        key_p = jnp.where(
            upper, pltpu.roll(key, distance, axis), pltpu.roll(key, size - distance, axis)
        )
        value_p = jnp.where(
            upper, pltpu.roll(value, distance, axis), pltpu.roll(value, size - distance, axis)
        )
        gap = key_p - key
        take = jnp.where(largest, gap, -gap) > 0
        return jnp.where(take, key_p, key), jnp.where(take, value_p, value)

    def bit_of(array, bit):
        return ((array >> bit) & 1) == 1

    def registers(items, level, down):
        for bit in range(level, -1, -1):
            for low in range(16):
                if low & (1 << bit):
                    continue
                high = low | (1 << bit)
                order = down(low) if callable(down) else down
                items[low], items[high] = pair(items[low], items[high], order)
        return items

    def sublanes(items, bit, down):
        upper = bit_of(sublane, bit)
        largest = jnp.logical_xor(upper, down) if not isinstance(down, bool) else (
            jnp.logical_not(upper) if down else upper
        )
        return [within(item, 0, 1 << bit, upper, largest) for item in items]

    def load(group):
        return [(keys[group * 16 + i], values[group * 16 + i]) for i in range(16)]

    def store(group, items):
        for i, (key, value) in enumerate(items):
            keys[group * 16 + i] = key
            values[group * 16 + i] = value

    for group in range(2):
        items = load(group)
        for level in range(1, 4):
            items = registers(
                items, level - 1, lambda low, level=level: bool((low >> level) & 1)
            )
        items = registers(items, 3, bit_of(sublane, 0))
        for level in range(1, 3):
            down = bit_of(sublane, level)
            for bit in range(level - 1, -1, -1):
                items = sublanes(items, bit, down)
            items = registers(items, 3, down)
        down = bool(group)
        for bit in range(2, -1, -1):
            items = sublanes(items, bit, down)
        items = registers(items, 3, down)
        store(group, items)

    def merge(level, carry):
        down = ((lane >> level) & 1) == 1

        def across(turn, inner):
            bit = level - 1 - turn
            distance = jnp.int32(1) << bit
            upper = ((lane >> bit) & 1) == 1
            largest = jnp.logical_xor(upper, down)
            for i in range(32):
                keys[i], values[i] = within((keys[i], values[i]), 1, distance, upper, largest)
            return inner

        lax.fori_loop(0, level, across, 0)
        for i in range(16):
            low, high = pair((keys[i], values[i]), (keys[i + 16], values[i + 16]), down)
            keys[i], values[i] = low
            keys[i + 16], values[i + 16] = high
        for group in range(2):
            items = load(group)
            for bit in range(2, -1, -1):
                items = sublanes(items, bit, down)
            items = registers(items, 3, down)
            store(group, items)
        return carry

    lax.fori_loop(0, 8, merge, 0)

    for half in range(2):
        part = keys[pl.ds(half * 16, 16)].reshape(LANES, LANES)
        keys_out[pl.ds(half, LANES, 2), :] = part.T
        part = values[pl.ds(half * 16, 16)].reshape(LANES, LANES)
        values_out[pl.ds(half, LANES, 2), :] = part.T
    keys_out[2 * LANES :, :] = jnp.full((8, LANES), -1, jnp.int32)
    values_out[2 * LANES :, :] = jnp.zeros((8, LANES), jnp.float32)
    for copy in near:
        copy.wait()


def sort_probes(offset, depth, row, column, step_of, observed, planes, rate, state):
    count = depth.size
    shape = (count // LANES, LANES)
    vmem = pl.BlockSpec(memory_space=pltpu.VMEM)
    smem = pl.BlockSpec(memory_space=pltpu.SMEM)
    stay = pl.BlockSpec(memory_space=pl.ANY)
    return pl.pallas_call(
        sort_kernel,
        out_shape=(
            jax.ShapeDtypeStruct((shape[0] + 8, LANES), jnp.int32),
            jax.ShapeDtypeStruct((shape[0] + 8, LANES), jnp.float32),
            jax.ShapeDtypeStruct((planes + 1,), jnp.int32),
            jax.ShapeDtypeStruct(rate.shape, jnp.float32),
            jax.ShapeDtypeStruct(state.shape, jnp.float32),
        ),
        in_specs=[smem] + [vmem] * 5 + [stay] * 2,
        out_specs=(vmem, vmem, smem, stay, stay),
        scratch_shapes=[
            pltpu.VMEM((shape[0] // 8, 8, LANES), jnp.int32),
            pltpu.VMEM((shape[0] // 8, 8, LANES), jnp.float32),
            pltpu.SemaphoreType.DMA((2,)),
        ],
        compiler_params=pltpu.CompilerParams(vmem_limit_bytes=42 * 2**20),
        cost_estimate=pl.CostEstimate(flops=20_000_000, bytes_accessed=2**20, transcendentals=0),
        name="sort_probes",
    )(offset, *(a.reshape(shape) for a in (depth, row, column, step_of, observed)), rate, state)


def bin_kernel(starts, keys_ref, values_ref, *fields):
    place = pl.program_id(0)
    size = fields[0].shape[1]
    both = STEPS * size
    counts, sums = fields[:STEPS], fields[STEPS:]
    begin, end = starts[place], starts[place + 1]
    first = begin >> 7
    windows = (end - (first << 7) + 2 * LANES - 1) >> 8

    def window(turn):
        at = first + 2 * turn
        key = jnp.concatenate([keys_ref[pl.ds(at, 1), :], keys_ref[pl.ds(at + 1, 1), :]], axis=1)
        value = jnp.concatenate(
            [values_ref[pl.ds(at, 1), :], values_ref[pl.ds(at + 1, 1), :]], axis=1
        )
        target = lax.broadcasted_iota(jnp.int32, (both, 2 * LANES), 0) + (place << 9)
        in_row = jnp.where((key >> 8) == target, 1.0, 0.0).astype(jnp.bfloat16)
        in_column = (key & 255) == lax.broadcasted_iota(jnp.int32, (size, 2 * LANES), 0)
        coarse = value.astype(jnp.bfloat16).astype(jnp.float32)
        rest = value - coarse

        def product(amount):
            return lax.dot_general(
                in_row,
                jnp.where(in_column, amount, 0.0).astype(jnp.bfloat16),
                (((1,), (1,)), ((), ())),
                preferred_element_type=jnp.float32,
            )

        return product(1.0), product(coarse) + product(rest)

    def parts(pair):
        for fields_of, values in zip((counts, sums), pair):
            for step, field in enumerate(fields_of):
                yield field, values[step * size : (step + 1) * size]

    for field, value in parts(window(0)):
        field[0] = value

    def more(turn, carry):
        for field, value in parts(window(turn)):
            field[0] += value
        return carry

    lax.fori_loop(1, windows, more, 0)


def bin_probes(starts, keys, values, rows_count, cols_count):
    places = starts.shape[0] - 1
    vmem = pl.BlockSpec(memory_space=pltpu.VMEM)
    block = pl.BlockSpec((1, rows_count, cols_count), lambda i: (i, 0, 0))
    field = jax.ShapeDtypeStruct((places, rows_count, cols_count), jnp.float32)
    return pl.pallas_call(
        bin_kernel,
        grid=(places,),
        out_shape=(field,) * (2 * STEPS),
        in_specs=[pl.BlockSpec(memory_space=pltpu.SMEM), vmem, vmem],
        out_specs=(block,) * (2 * STEPS),
        compiler_params=pltpu.CompilerParams(
            vmem_limit_bytes=5 * 2**20, dimension_semantics=("arbitrary",)
        ),
        cost_estimate=pl.CostEstimate(
            flops=30_000_000, bytes_accessed=20 * 2**20, transcendentals=0
        ),
        name="bin_probes",
    )(starts, keys, values)


def ahead(parts):
    lane = lax.broadcasted_iota(jnp.int32, parts[0].shape, 1)
    left, right = (pltpu.roll(part, LANES - 1, 1) for part in parts)
    last = lane == LANES - 1
    return jnp.where(last, right, left), jnp.where(last, left, right)


def behind(parts):
    lane = lax.broadcasted_iota(jnp.int32, parts[0].shape, 1)
    left, right = (pltpu.roll(part, 1, 1) for part in parts)
    first = lane == 0
    return jnp.where(first, right, left), jnp.where(first, left, right)


def sweep_kernel(
    source_plane,
    rate_low,
    rate_own,
    rate_high,
    state_low,
    state_own,
    state_high,
    velocity_ref,
    profile_ref,
    count1,
    count2,
    sum1,
    sum2,
    columns_table,
    out_ref,
    half_rate,
    state0,
    state1,
    adjoint2,
    adjoint1,
    face_x,
    grad_x0,
    grad_x1,
    grad_x2,
    inject1,
    depth_product,
    pair_sum,
    coarse_rows,
):
    index = pl.program_id(0)
    total = pl.num_programs(0)
    size = half_rate.shape[2] - 2 * PAD
    halves = range(2)
    strips = range(0, size, STRIP)

    def rows(ref, plane, half, start, shift=0):
        slot = plane & (ref.shape[0] - 1)
        return ref[slot, half, PAD + start + shift : PAD + start + shift + STRIP, :]

    def put(ref, plane, half, start, value):
        slot = plane & (ref.shape[0] - 1)
        ref[slot, half, PAD + start : PAD + start + STRIP, :] = value
        if start == 0:
            ref[slot, half, PAD + size : PAD + size + 1, :] = value[:1]
        if start + STRIP == size:
            ref[slot, half, PAD - 1 : PAD, :] = value[STRIP - 1 :]

    def plain(ref, plane, half, start):
        return ref[plane & (ref.shape[0] - 1), half, start : start + STRIP, :]

    def put_plain(ref, plane, half, start, value):
        ref[plane & (ref.shape[0] - 1), half, start : start + STRIP, :] = value

    def enter(rate_ref, state_ref):
        for start in strips:
            span = slice(start, start + STRIP)
            rate, state = [], []
            for half in halves:
                cols = slice(half * LANES, (half + 1) * LANES)
                rate.append((0.5 * TIME_STEP) * jnp.exp(rate_ref[0, span, cols]))
                state.append(state_ref[0, span, cols])
            rate_ahead, state_ahead = ahead(rate), ahead(state)
            for half in halves:
                put(half_rate, index, half, start, rate[half])
                put(state0, index, half, start, state[half])
                put_plain(face_x, index, half, start, rate[half] + rate_ahead[half])
                put_plain(grad_x0, index, half, start, state_ahead[half] - state[half])

    @pl.when(index < HALO)
    def _():
        enter(rate_low, state_low)

    @pl.when((index >= HALO) & (index < total - HALO))
    def _():
        enter(rate_own, state_own)

    @pl.when((index >= total - HALO) & (index < total))
    def _():
        enter(rate_high, state_high)

    def advance(field, grad_x, slot, start, adjoint):
        up, down = slot + 1, slot - 1
        flux = [
            plain(face_x, slot, half, start) * plain(grad_x, slot, half, start) for half in halves
        ]
        flux_behind = behind(flux)
        result = []
        for half in halves:
            value = rows(field, slot, half, start)
            rate = rows(half_rate, slot, half, start)
            wind = TIME_STEP * velocity_ref[
                start : start + STRIP, half * LANES : (half + 1) * LANES
            ]
            rate_up = rate + rows(half_rate, up, half, start)
            rate_down = rate + rows(half_rate, down, half, start)
            if adjoint:
                rate_up = rate_up + wind
            else:
                rate_down = rate_down + wind
            depth_part = rate_up * (rows(field, up, half, start) - value) - rate_down * (
                value - rows(field, down, half, start)
            )
            row_part = (rate + rows(half_rate, slot, half, start, 1)) * (
                rows(field, slot, half, start, 1) - value
            ) - (rate + rows(half_rate, slot, half, start, -1)) * (
                value - rows(field, slot, half, start, -1)
            )
            result.append(value + depth_part + row_part + (flux[half] - flux_behind[half]))
        return result

    def save(field, grad_x, slot, start, parts):
        parts_ahead = ahead(parts)
        for half in halves:
            put(field, slot, half, start, parts[half])
            put_plain(grad_x, slot, half, start, parts_ahead[half] - parts[half])

    def source_gain(plane):
        return jnp.where(plane == source_plane[0], jnp.float32(TIME_STEP), jnp.float32(0.0))

    def source(gain, half, start):
        return gain * profile_ref[0, start : start + STRIP, half * LANES : (half + 1) * LANES]

    plane1 = index - 1

    @pl.when((plane1 >= 1) & (plane1 < total - 1))
    def _():
        slot = plane1
        gain = source_gain(plane1)
        for start in strips:
            parts = advance(state0, grad_x0, slot, start, False)
            parts = [parts[half] + source(gain, half, start) for half in halves]
            save(state1, grad_x1, slot, start, parts)

    plane2 = index - 2

    @pl.when((plane2 >= 2) & (plane2 < total - 2))
    def _():
        slot = plane2
        gain = source_gain(plane2)
        for start in strips:
            parts = advance(state1, grad_x1, slot, start, False)
            mu = []
            for half in halves:
                cols = slice(half * LANES, (half + 1) * LANES)
                state2 = parts[half] + source(gain, half, start)
                span = slice(start, start + STRIP)
                mu.append(count2[0, span, cols] * state2 - sum2[0, span, cols])
                put_plain(
                    inject1,
                    slot,
                    half,
                    start,
                    count1[0, span, cols] * rows(state1, slot, half, start) - sum1[0, span, cols],
                )
            save(adjoint2, grad_x2, slot, start, mu)

    plane3 = index - 3

    @pl.when((plane3 >= 3) & (plane3 < total - 3))
    def _():
        slot = plane3
        for start in strips:
            parts = advance(adjoint2, grad_x2, slot, start, True)
            for half in halves:
                put(
                    adjoint1,
                    slot,
                    half,
                    start,
                    parts[half] + plain(inject1, slot, half, start),
                )

    plane4 = index - 4

    def products(slot, other, half, start):
        def step(field):
            return rows(field, other, half, start) - rows(field, slot, half, start)

        return step(state0) * step(adjoint1) + step(state1) * step(adjoint2)

    @pl.when(plane4 == HALO - 1)
    def _():
        slot = plane4
        for start in strips:
            for half in halves:
                depth_product[half, start : start + STRIP, :] = products(
                    slot, slot + 1, half, start
                )

    @pl.when(plane4 >= HALO)
    def _():
        slot, up = plane4, plane4 + 1
        even = (plane4 & 1) == 0
        for start in strips:
            mu = [rows(adjoint1, slot, half, start) for half in halves]
            mu_ahead = ahead(mu)
            product_x = [
                plain(grad_x0, slot, half, start) * (mu_ahead[half] - mu[half])
                + plain(grad_x1, slot, half, start) * plain(grad_x2, slot, half, start)
                for half in halves
            ]
            product_behind = behind(product_x)
            for half in halves:
                span = slice(start, start + STRIP)
                result = product_x[half] + product_behind[half]
                upper = products(slot, up, half, start)
                result = result + (upper + depth_product[half, span, :])
                depth_product[half, span, :] = upper
                for shift in (1, -1):
                    factors = [
                        rows(field, slot, half, start, shift) - rows(field, slot, half, start)
                        for field in (state0, adjoint1, state1, adjoint2)
                    ]
                    result = result + (factors[0] * factors[1] + factors[2] * factors[3])
                result = -rows(half_rate, slot, half, start) * result
                pair_sum[half, span, :] = jnp.where(even, 0.0, pair_sum[half, span, :]) + result

    @pl.when((plane4 >= HALO) & ((plane4 & 1) == 1))
    def _():
        for half in halves:
            even_rows = pair_sum[half, pl.ds(0, size // R, R), :]
            odd_rows = pair_sum[half, pl.ds(1, size // R, R), :]
            cols = slice(half * LANES, (half + 1) * LANES)
            coarse_rows[(plane4 - HALO) >> 1, :, cols] = even_rows + odd_rows

    @pl.when(index == total - 1)
    def _():
        planes = coarse_rows.shape[0]
        for plane in range(planes):
            out_ref[pl.ds(plane, columns_table.shape[0], planes), :] = lax.dot_general(
                columns_table[...],
                coarse_rows[plane],
                (((1,), (1,)), ((), ())),
                precision=lax.Precision.HIGHEST,
                preferred_element_type=jnp.float32,
            )


def sweep(source_plane, rates, states, velocity, profile, fields):
    own, rows_count, cols_count = rates[1].shape
    total = own + 2 * HALO
    coarse = rows_count // R
    plane = (1, rows_count, cols_count)
    smem = pl.BlockSpec(memory_space=pltpu.SMEM)
    vmem = pl.BlockSpec(memory_space=pltpu.VMEM)
    low = pl.BlockSpec(plane, lambda i: (jnp.minimum(i, HALO - 1), 0, 0))
    middle = pl.BlockSpec(plane, lambda i: (jnp.clip(i - HALO, 0, own - 1), 0, 0))
    high = pl.BlockSpec(plane, lambda i: (jnp.clip(i - HALO - own, 0, HALO - 1), 0, 0))
    columns_table = jnp.asarray(np.repeat(hartley(cols_count // R), R, axis=1))
    voxels = pl.BlockSpec(
        (1, rows_count, cols_count),
        lambda i: (jnp.clip(i - HALO, 0, total - 2 * LEAD - 1), 0, 0),
    )
    def padded(kept):
        return pltpu.VMEM((kept, 2, rows_count + 2 * PAD, LANES), jnp.float32)

    def plain(kept):
        return pltpu.VMEM((kept, 2, rows_count, LANES), jnp.float32)

    return pl.pallas_call(
        sweep_kernel,
        grid=(total,),
        out_shape=jax.ShapeDtypeStruct((cols_count // R * (own // R), coarse), jnp.float32),
        in_specs=[smem, low, middle, high, low, middle, high, vmem, vmem] + [voxels] * 4 + [vmem],
        out_specs=vmem,
        scratch_shapes=[padded(LONG)] * 2
        + [padded(SHORT)] * 3
        + [plain(SHORT), plain(LONG), plain(SHORT), plain(SHORT), plain(2)]
        + [
            pltpu.VMEM((2, rows_count, LANES), jnp.float32),
            pltpu.VMEM((2, rows_count, LANES), jnp.float32),
            pltpu.VMEM((own // R, coarse, cols_count), jnp.float32),
        ],
        compiler_params=pltpu.CompilerParams(
            vmem_limit_bytes=18 * 2**20, dimension_semantics=("arbitrary",)
        ),
        cost_estimate=pl.CostEstimate(
            flops=200_000_000, bytes_accessed=34 * 2**20, transcendentals=0
        ),
        name="sweep",
    )(
        source_plane,
        *rates,
        *states,
        velocity,
        profile,
        *fields,
        columns_table,
    )


def exact_dot(a, b):
    return jnp.dot(a, b, precision=lax.Precision.HIGHEST, preferred_element_type=jnp.float32)


def filter_kernel(lam_second, received, table_ref, symbol_depth, symbol_rows, out_ref, field):
    depth_blocks, tracers, planes, size = received.shape
    for block in range(depth_blocks):
        field[block * planes : (block + 1) * planes, :] = jnp.sum(received[block], axis=0)
    table = table_ref[...]
    spectrum = exact_dot(exact_dot(table, field[...]), table)
    lam = symbol_depth[...] + symbol_rows[...] + lam_second[0]
    factor = 1.0 + PRIOR_RANGE * lam
    spectrum = spectrum * (1.0 / (factor * factor) / float(size**3))
    field[...] = exact_dot(exact_dot(table, spectrum), table)
    share = size // tracers
    group = lax.broadcasted_iota(jnp.int32, (depth_blocks, size), 1) // share
    by_plane = [field[pl.ds(plane, depth_blocks, planes), :] for plane in range(planes)]
    for tracer in range(tracers):
        part = jnp.zeros((depth_blocks, size), jnp.float32)
        for plane in range(planes):
            shift = (plane - tracer) * share % size
            moved = pltpu.roll(by_plane[plane], shift, 1) if shift else by_plane[plane]
            part = jnp.where(group == plane, moved, part)
        out_ref[pl.ds(tracer, depth_blocks, tracers), :] = part


def filtered(received, own_symbol):
    depth_blocks, tracers, planes, size = received.shape
    line = symbol(size)
    vmem = pl.BlockSpec(memory_space=pltpu.VMEM)
    return pl.pallas_call(
        filter_kernel,
        out_shape=jax.ShapeDtypeStruct((depth_blocks * tracers, size), jnp.float32),
        in_specs=[pl.BlockSpec(memory_space=pltpu.SMEM)] + [vmem] * 4,
        out_specs=vmem,
        scratch_shapes=[pltpu.VMEM((depth_blocks * planes, size), jnp.float32)],
        compiler_params=pltpu.CompilerParams(vmem_limit_bytes=16 * 2**20),
        name="filter",
    )(
        own_symbol,
        received,
        jnp.asarray(hartley(size)),
        jnp.asarray(line[:, None]),
        jnp.asarray(line[None, :]),
    )


def inverse_kernel(received, table_ref, out_ref):
    out_ref[...] = lax.dot_general(
        received[...],
        table_ref[...],
        (((0,), (0,)), ((), ())),
        precision=lax.Precision.HIGHEST,
        preferred_element_type=jnp.float32,
    )


def inverse_columns(received):
    vmem = pl.BlockSpec(memory_space=pltpu.VMEM)
    return pl.pallas_call(
        inverse_kernel,
        out_shape=jax.ShapeDtypeStruct(received.shape, jnp.float32),
        in_specs=[vmem, vmem],
        out_specs=vmem,
        compiler_params=pltpu.CompilerParams(vmem_limit_bytes=16 * 2**20),
        name="inverse_columns",
    )(received, jnp.asarray(hartley(received.shape[0])))


def neighbours(first, last):
    count = lax.axis_size("domain")
    up = [(i, (i + 1) % count) for i in range(count)]
    down = [(j, i) for i, j in up]
    return lax.ppermute(last, "domain", up), lax.ppermute(first, "domain", down)


def local(log_rate, velocity, initial, profile, plane, depth, row, column, step_of, observed):
    slab, rows_count, cols_count = log_rate.shape
    domain_count, tracer_count = lax.axis_size("domain"), lax.axis_size("tracer")
    full = slab * domain_count
    offset = lax.axis_index("domain") * slab
    rate_low, rate_high = neighbours(log_rate[:HALO], log_rate[-HALO:])
    state_low, state_high = neighbours(initial[0, :HALO], initial[0, -HALO:])
    keys, values, starts, rate_near, state_near = sort_probes(
        offset.astype(jnp.int32)[None],
        depth,
        row,
        column,
        step_of,
        observed,
        slab + 2 * LEAD,
        log_rate,
        initial[0],
    )
    source_plane = (plane - (offset - HALO)) % full
    fields = bin_probes(starts, keys, values, rows_count, cols_count)
    rates = (rate_low, rate_near, rate_high)
    states = (state_low, state_near, state_high)
    spectral = sweep(source_plane, rates, states, velocity, profile, fields)
    first, planes, second = rows_count // R, slab // R, cols_count // R
    axes = ("domain", "tracer")
    received = lax.all_to_all(
        spectral.reshape(second, planes, first), axes, split_axis=0, concat_axis=0, tiled=True
    )
    own = lax.axis_index("domain") * tracer_count + lax.axis_index("tracer")
    own_symbol = lax.dynamic_slice(jnp.asarray(symbol(second)), (own,), (1,))
    back = filtered(received.reshape(domain_count, tracer_count, planes, first), own_symbol)
    result = lax.all_to_all(back, axes, split_axis=0, concat_axis=0, tiled=True)
    return inverse_columns(result).reshape(planes, first // tracer_count, second)


def solution(mesh):
    return jax.shard_map(
        local,
        mesh=mesh,
        in_specs=(
            P("domain", None, None),
            P(),
            P("tracer", "domain", None, None),
            P("tracer", None, None),
            P("tracer"),
            P("tracer", None),
            P("tracer", None),
            P("tracer", None),
            P("tracer", None),
            P("tracer", None),
        ),
        out_specs=P("domain", "tracer", None),
        check_vma=False,
    )
```

```python
import functools
import math

import jax
import jax.numpy as jnp
import numpy as np
from jax import lax
from jax.experimental import pallas as pl
from jax.experimental.pallas import tpu as pltpu
from jax.sharding import PartitionSpec as P

R = 2
STEPS = 2
TIME_STEP = 0.14
PRIOR_RANGE = 4.0

HALO = 4
LEAD = 2
LANES = 128
LONG, SHORT = 8, 4
PAD = 8
STRIP = 32


def hartley(length):
    phases = np.outer(np.arange(length), np.arange(length)) % length
    angles = 2.0 * math.pi / length * phases
    return (np.cos(angles) + np.sin(angles)).astype(np.float32)


def symbol(length):
    return (2.0 - 2.0 * np.cos(2.0 * math.pi / length * np.arange(length))).astype(np.float32)


def sort_kernel(
    offset_ref,
    depth_far,
    row_far,
    column_far,
    step_far,
    observed_far,
    rate,
    state,
    keys_out,
    values_out,
    starts_out,
    rate_near,
    state_near,
    keys,
    values,
    depth_ref,
    row_ref,
    column_ref,
    step_ref,
    observed_ref,
    sems,
):
    probes = [
        pltpu.make_async_copy(far, near, sems.at[2 + at])
        for at, (far, near) in enumerate(
            (
                (depth_far, depth_ref),
                (row_far, row_ref),
                (column_far, column_ref),
                (step_far, step_ref),
                (observed_far, observed_ref),
            )
        )
    ]
    for copy in probes:
        copy.start()
    near = [
        pltpu.make_async_copy(rate, rate_near, sems.at[0]),
        pltpu.make_async_copy(state, state_near, sems.at[1]),
    ]
    for copy in near:
        copy.start()
    for copy in probes:
        copy.wait()
    offset = offset_ref[0]
    plane = (depth_ref[...] - (offset - LEAD)) & 255
    key = (plane << 17) | ((step_ref[...] - 1) << 16) | (row_ref[...] << 8) | column_ref[...]
    keys[...] = key.reshape(keys.shape)
    values[...] = observed_ref[...].reshape(values.shape)
    for index in range(starts_out.shape[0]):
        if index == 0:
            starts_out[index] = 0
        else:
            starts_out[index] = jnp.sum((key < (index << 17)).astype(jnp.int32))

    lane = lax.broadcasted_iota(jnp.int32, (8, LANES), 1)
    sublane = lax.broadcasted_iota(jnp.int32, (8, LANES), 0)

    def pair(low, high, down):
        (key_a, value_a), (key_b, value_b) = low, high
        if down is False:
            swap = key_a > key_b
        elif down is True:
            swap = key_a < key_b
        else:
            swap = jnp.logical_xor(key_a > key_b, down)
        return (
            (jnp.where(swap, key_b, key_a), jnp.where(swap, value_b, value_a)),
            (jnp.where(swap, key_a, key_b), jnp.where(swap, value_a, value_b)),
        )

    def within(item, axis, distance, upper, largest):
        key, value = item
        size = key.shape[axis]
        key_p = jnp.where(
            upper, pltpu.roll(key, distance, axis), pltpu.roll(key, size - distance, axis)
        )
        value_p = jnp.where(
            upper, pltpu.roll(value, distance, axis), pltpu.roll(value, size - distance, axis)
        )
        gap = key_p - key
        take = jnp.where(largest, gap, -gap) > 0
        return jnp.where(take, key_p, key), jnp.where(take, value_p, value)

    def bit_of(array, bit):
        return ((array >> bit) & 1) == 1

    def registers(items, level, down):
        for bit in range(level, -1, -1):
            for low in range(16):
                if low & (1 << bit):
                    continue
                high = low | (1 << bit)
                order = down(low) if callable(down) else down
                items[low], items[high] = pair(items[low], items[high], order)
        return items

    def sublanes(items, bit, down):
        upper = bit_of(sublane, bit)
        largest = jnp.logical_xor(upper, down) if not isinstance(down, bool) else (
            jnp.logical_not(upper) if down else upper
        )
        return [within(item, 0, 1 << bit, upper, largest) for item in items]

    def load(group):
        return [(keys[group * 16 + i], values[group * 16 + i]) for i in range(16)]

    def store(group, items):
        for i, (key, value) in enumerate(items):
            keys[group * 16 + i] = key
            values[group * 16 + i] = value

    for group in range(2):
        items = load(group)
        for level in range(1, 4):
            items = registers(
                items, level - 1, lambda low, level=level: bool((low >> level) & 1)
            )
        items = registers(items, 3, bit_of(sublane, 0))
        for level in range(1, 3):
            down = bit_of(sublane, level)
            for bit in range(level - 1, -1, -1):
                items = sublanes(items, bit, down)
            items = registers(items, 3, down)
        down = bool(group)
        for bit in range(2, -1, -1):
            items = sublanes(items, bit, down)
        items = registers(items, 3, down)
        store(group, items)

    def merge(level, carry):
        down = ((lane >> level) & 1) == 1

        def across(turn, inner):
            bit = level - 1 - turn
            distance = jnp.int32(1) << bit
            upper = ((lane >> bit) & 1) == 1
            largest = jnp.logical_xor(upper, down)
            for i in range(32):
                keys[i], values[i] = within((keys[i], values[i]), 1, distance, upper, largest)
            return inner

        lax.fori_loop(0, level, across, 0)
        for i in range(16):
            low, high = pair((keys[i], values[i]), (keys[i + 16], values[i + 16]), down)
            keys[i], values[i] = low
            keys[i + 16], values[i + 16] = high
        for group in range(2):
            items = load(group)
            for bit in range(2, -1, -1):
                items = sublanes(items, bit, down)
            items = registers(items, 3, down)
            store(group, items)
        return carry

    lax.fori_loop(0, 8, merge, 0)

    for half in range(2):
        part = keys[pl.ds(half * 16, 16)].reshape(LANES, LANES)
        keys_out[pl.ds(half, LANES, 2), :] = part.T
        part = values[pl.ds(half * 16, 16)].reshape(LANES, LANES)
        values_out[pl.ds(half, LANES, 2), :] = part.T
    keys_out[2 * LANES :, :] = jnp.full((8, LANES), -1, jnp.int32)
    values_out[2 * LANES :, :] = jnp.zeros((8, LANES), jnp.float32)
    for copy in near:
        copy.wait()


def sort_probes(offset, depth, row, column, step_of, observed, planes, rate, state):
    count = depth.size
    shape = (count // LANES, LANES)
    vmem = pl.BlockSpec(memory_space=pltpu.VMEM)
    smem = pl.BlockSpec(memory_space=pltpu.SMEM)
    stay = pl.BlockSpec(memory_space=pl.ANY)
    return pl.pallas_call(
        sort_kernel,
        out_shape=(
            jax.ShapeDtypeStruct((shape[0] + 8, LANES), jnp.int32),
            jax.ShapeDtypeStruct((shape[0] + 8, LANES), jnp.float32),
            jax.ShapeDtypeStruct((planes + 1,), jnp.int32),
            jax.ShapeDtypeStruct(rate.shape, jnp.float32),
            jax.ShapeDtypeStruct(state.shape, jnp.float32),
        ),
        in_specs=[smem] + [stay] * 7,
        out_specs=(vmem, vmem, smem, stay, stay),
        scratch_shapes=[
            pltpu.VMEM((shape[0] // 8, 8, LANES), jnp.int32),
            pltpu.VMEM((shape[0] // 8, 8, LANES), jnp.float32),
            *[pltpu.VMEM(shape, jnp.int32)] * 4,
            pltpu.VMEM(shape, jnp.float32),
            pltpu.SemaphoreType.DMA((7,)),
        ],
        compiler_params=pltpu.CompilerParams(vmem_limit_bytes=42 * 2**20),
        cost_estimate=pl.CostEstimate(flops=20_000_000, bytes_accessed=2**20, transcendentals=0),
        name="sort_probes",
    )(offset, *(a.reshape(shape) for a in (depth, row, column, step_of, observed)), rate, state)


def bin_kernel(starts, keys_ref, values_ref, *fields):
    place = pl.program_id(0)
    size = fields[0].shape[1]
    both = STEPS * size
    counts, sums = fields[:STEPS], fields[STEPS:]
    begin, end = starts[place], starts[place + 1]
    first = begin >> 7
    windows = (end - (first << 7) + 2 * LANES - 1) >> 8

    def window(turn):
        at = first + 2 * turn
        key = jnp.concatenate([keys_ref[pl.ds(at, 1), :], keys_ref[pl.ds(at + 1, 1), :]], axis=1)
        value = jnp.concatenate(
            [values_ref[pl.ds(at, 1), :], values_ref[pl.ds(at + 1, 1), :]], axis=1
        )
        target = lax.broadcasted_iota(jnp.int32, (both, 2 * LANES), 0) + (place << 9)
        in_row = jnp.where((key >> 8) == target, 1.0, 0.0).astype(jnp.bfloat16)
        in_column = (key & 255) == lax.broadcasted_iota(jnp.int32, (size, 2 * LANES), 0)
        coarse = value.astype(jnp.bfloat16).astype(jnp.float32)
        rest = value - coarse

        def product(amount):
            return lax.dot_general(
                in_row,
                jnp.where(in_column, amount, 0.0).astype(jnp.bfloat16),
                (((1,), (1,)), ((), ())),
                preferred_element_type=jnp.float32,
            )

        return product(1.0), product(coarse) + product(rest)

    def parts(pair):
        for fields_of, values in zip((counts, sums), pair):
            for step, field in enumerate(fields_of):
                yield field, values[step * size : (step + 1) * size]

    for field, value in parts(window(0)):
        field[0] = value

    def more(turn, carry):
        for field, value in parts(window(turn)):
            field[0] += value
        return carry

    lax.fori_loop(1, windows, more, 0)


def bin_probes(starts, keys, values, rows_count, cols_count):
    places = starts.shape[0] - 1
    vmem = pl.BlockSpec(memory_space=pltpu.VMEM)
    block = pl.BlockSpec((1, rows_count, cols_count), lambda i: (i, 0, 0))
    field = jax.ShapeDtypeStruct((places, rows_count, cols_count), jnp.float32)
    return pl.pallas_call(
        bin_kernel,
        grid=(places,),
        out_shape=(field,) * (2 * STEPS),
        in_specs=[pl.BlockSpec(memory_space=pltpu.SMEM), vmem, vmem],
        out_specs=(block,) * (2 * STEPS),
        compiler_params=pltpu.CompilerParams(
            vmem_limit_bytes=5 * 2**20, dimension_semantics=("arbitrary",)
        ),
        cost_estimate=pl.CostEstimate(
            flops=30_000_000, bytes_accessed=20 * 2**20, transcendentals=0
        ),
        name="bin_probes",
    )(starts, keys, values)


def ahead(parts):
    lane = lax.broadcasted_iota(jnp.int32, parts[0].shape, 1)
    left, right = (pltpu.roll(part, LANES - 1, 1) for part in parts)
    last = lane == LANES - 1
    return jnp.where(last, right, left), jnp.where(last, left, right)


def behind(parts):
    lane = lax.broadcasted_iota(jnp.int32, parts[0].shape, 1)
    left, right = (pltpu.roll(part, 1, 1) for part in parts)
    first = lane == 0
    return jnp.where(first, right, left), jnp.where(first, left, right)


def sweep_kernel(
    source_plane,
    rate_low,
    rate_own,
    rate_high,
    state_low,
    state_own,
    state_high,
    velocity_ref,
    profile_ref,
    count1,
    count2,
    sum1,
    sum2,
    columns_table,
    out_ref,
    half_rate,
    state0,
    state1,
    adjoint2,
    adjoint1,
    face_x,
    grad_x0,
    grad_x1,
    grad_x2,
    inject1,
    depth_product,
    pair_sum,
    coarse_rows,
):
    index = pl.program_id(0)
    total = pl.num_programs(0)
    size = half_rate.shape[2] - 2 * PAD
    halves = range(2)
    strips = range(0, size, STRIP)

    def rows(ref, plane, half, start, shift=0):
        slot = plane & (ref.shape[0] - 1)
        return ref[slot, half, PAD + start + shift : PAD + start + shift + STRIP, :]

    def put(ref, plane, half, start, value):
        slot = plane & (ref.shape[0] - 1)
        ref[slot, half, PAD + start : PAD + start + STRIP, :] = value
        if start == 0:
            ref[slot, half, PAD + size : PAD + size + 1, :] = value[:1]
        if start + STRIP == size:
            ref[slot, half, PAD - 1 : PAD, :] = value[STRIP - 1 :]

    def plain(ref, plane, half, start):
        return ref[plane & (ref.shape[0] - 1), half, start : start + STRIP, :]

    def put_plain(ref, plane, half, start, value):
        ref[plane & (ref.shape[0] - 1), half, start : start + STRIP, :] = value

    def enter(rate_ref, state_ref):
        for start in strips:
            span = slice(start, start + STRIP)
            rate, state = [], []
            for half in halves:
                cols = slice(half * LANES, (half + 1) * LANES)
                rate.append((0.5 * TIME_STEP) * jnp.exp(rate_ref[0, span, cols]))
                state.append(state_ref[0, span, cols])
            rate_ahead, state_ahead = ahead(rate), ahead(state)
            for half in halves:
                put(half_rate, index, half, start, rate[half])
                put(state0, index, half, start, state[half])
                put_plain(face_x, index, half, start, rate[half] + rate_ahead[half])
                put_plain(grad_x0, index, half, start, state_ahead[half] - state[half])

    @pl.when(index < HALO)
    def _():
        enter(rate_low, state_low)

    @pl.when((index >= HALO) & (index < total - HALO))
    def _():
        enter(rate_own, state_own)

    @pl.when((index >= total - HALO) & (index < total))
    def _():
        enter(rate_high, state_high)

    def advance(field, grad_x, slot, start, adjoint):
        up, down = slot + 1, slot - 1
        flux = [
            plain(face_x, slot, half, start) * plain(grad_x, slot, half, start) for half in halves
        ]
        flux_behind = behind(flux)
        result = []
        for half in halves:
            value = rows(field, slot, half, start)
            rate = rows(half_rate, slot, half, start)
            wind = TIME_STEP * velocity_ref[
                start : start + STRIP, half * LANES : (half + 1) * LANES
            ]
            rate_up = rate + rows(half_rate, up, half, start)
            rate_down = rate + rows(half_rate, down, half, start)
            if adjoint:
                rate_up = rate_up + wind
            else:
                rate_down = rate_down + wind
            depth_part = rate_up * (rows(field, up, half, start) - value) - rate_down * (
                value - rows(field, down, half, start)
            )
            row_part = (rate + rows(half_rate, slot, half, start, 1)) * (
                rows(field, slot, half, start, 1) - value
            ) - (rate + rows(half_rate, slot, half, start, -1)) * (
                value - rows(field, slot, half, start, -1)
            )
            result.append(value + depth_part + row_part + (flux[half] - flux_behind[half]))
        return result

    def save(field, grad_x, slot, start, parts):
        parts_ahead = ahead(parts)
        for half in halves:
            put(field, slot, half, start, parts[half])
            put_plain(grad_x, slot, half, start, parts_ahead[half] - parts[half])

    def source_gain(plane):
        return jnp.where(plane == source_plane[0], jnp.float32(TIME_STEP), jnp.float32(0.0))

    def source(gain, half, start):
        return gain * profile_ref[0, start : start + STRIP, half * LANES : (half + 1) * LANES]

    plane1 = index - 1

    @pl.when((plane1 >= 1) & (plane1 < total - 1))
    def _():
        slot = plane1
        gain = source_gain(plane1)
        for start in strips:
            parts = advance(state0, grad_x0, slot, start, False)
            parts = [parts[half] + source(gain, half, start) for half in halves]
            save(state1, grad_x1, slot, start, parts)

    plane2 = index - 2

    @pl.when((plane2 >= 2) & (plane2 < total - 2))
    def _():
        slot = plane2
        gain = source_gain(plane2)
        for start in strips:
            parts = advance(state1, grad_x1, slot, start, False)
            mu = []
            for half in halves:
                cols = slice(half * LANES, (half + 1) * LANES)
                state2 = parts[half] + source(gain, half, start)
                span = slice(start, start + STRIP)
                mu.append(count2[0, span, cols] * state2 - sum2[0, span, cols])
                put_plain(
                    inject1,
                    slot,
                    half,
                    start,
                    count1[0, span, cols] * rows(state1, slot, half, start) - sum1[0, span, cols],
                )
            save(adjoint2, grad_x2, slot, start, mu)

    plane3 = index - 3

    @pl.when((plane3 >= 3) & (plane3 < total - 3))
    def _():
        slot = plane3
        for start in strips:
            parts = advance(adjoint2, grad_x2, slot, start, True)
            for half in halves:
                put(
                    adjoint1,
                    slot,
                    half,
                    start,
                    parts[half] + plain(inject1, slot, half, start),
                )

    plane4 = index - 4

    def products(slot, other, half, start):
        def step(field):
            return rows(field, other, half, start) - rows(field, slot, half, start)

        return step(state0) * step(adjoint1) + step(state1) * step(adjoint2)

    @pl.when(plane4 == HALO - 1)
    def _():
        slot = plane4
        for start in strips:
            for half in halves:
                depth_product[half, start : start + STRIP, :] = products(
                    slot, slot + 1, half, start
                )

    @pl.when(plane4 >= HALO)
    def _():
        slot, up = plane4, plane4 + 1
        even = (plane4 & 1) == 0
        for start in strips:
            mu = [rows(adjoint1, slot, half, start) for half in halves]
            mu_ahead = ahead(mu)
            product_x = [
                plain(grad_x0, slot, half, start) * (mu_ahead[half] - mu[half])
                + plain(grad_x1, slot, half, start) * plain(grad_x2, slot, half, start)
                for half in halves
            ]
            product_behind = behind(product_x)
            for half in halves:
                span = slice(start, start + STRIP)
                result = product_x[half] + product_behind[half]
                upper = products(slot, up, half, start)
                result = result + (upper + depth_product[half, span, :])
                depth_product[half, span, :] = upper
                for shift in (1, -1):
                    factors = [
                        rows(field, slot, half, start, shift) - rows(field, slot, half, start)
                        for field in (state0, adjoint1, state1, adjoint2)
                    ]
                    result = result + (factors[0] * factors[1] + factors[2] * factors[3])
                result = -rows(half_rate, slot, half, start) * result
                pair_sum[half, span, :] = jnp.where(even, 0.0, pair_sum[half, span, :]) + result

    @pl.when((plane4 >= HALO) & ((plane4 & 1) == 1))
    def _():
        for half in halves:
            even_rows = pair_sum[half, pl.ds(0, size // R, R), :]
            odd_rows = pair_sum[half, pl.ds(1, size // R, R), :]
            cols = slice(half * LANES, (half + 1) * LANES)
            coarse_rows[(plane4 - HALO) >> 1, :, cols] = even_rows + odd_rows

    @pl.when(index == total - 1)
    def _():
        planes = coarse_rows.shape[0]
        for plane in range(planes):
            out_ref[pl.ds(plane, columns_table.shape[0], planes), :] = lax.dot_general(
                columns_table[...],
                coarse_rows[plane],
                (((1,), (1,)), ((), ())),
                precision=lax.Precision.HIGHEST,
                preferred_element_type=jnp.float32,
            )


def sweep(source_plane, rates, states, velocity, profile, fields):
    own, rows_count, cols_count = rates[1].shape
    total = own + 2 * HALO
    coarse = rows_count // R
    plane = (1, rows_count, cols_count)
    smem = pl.BlockSpec(memory_space=pltpu.SMEM)
    vmem = pl.BlockSpec(memory_space=pltpu.VMEM)

    def low(which):
        return pl.BlockSpec((None, *plane), lambda i: (which, jnp.minimum(i, HALO - 1), 0, 0))

    def high(which):
        return pl.BlockSpec(
            (None, *plane), lambda i: (which, jnp.clip(i - HALO - own, 0, HALO - 1), 0, 0)
        )

    middle = pl.BlockSpec(plane, lambda i: (jnp.clip(i - HALO, 0, own - 1), 0, 0))
    columns_table = jnp.asarray(np.repeat(hartley(cols_count // R), R, axis=1))
    voxels = pl.BlockSpec(
        (1, rows_count, cols_count),
        lambda i: (jnp.clip(i - HALO, 0, total - 2 * LEAD - 1), 0, 0),
    )
    def padded(kept):
        return pltpu.VMEM((kept, 2, rows_count + 2 * PAD, LANES), jnp.float32)

    def plain(kept):
        return pltpu.VMEM((kept, 2, rows_count, LANES), jnp.float32)

    return pl.pallas_call(
        sweep_kernel,
        grid=(total,),
        out_shape=jax.ShapeDtypeStruct((cols_count // R * (own // R), coarse), jnp.float32),
        in_specs=[smem, low(0), middle, high(0), low(1), middle, high(1), vmem, vmem] + [voxels] * 4 + [vmem],
        out_specs=vmem,
        scratch_shapes=[padded(LONG)] * 2
        + [padded(SHORT)] * 3
        + [plain(SHORT), plain(LONG), plain(SHORT), plain(SHORT), plain(2)]
        + [
            pltpu.VMEM((2, rows_count, LANES), jnp.float32),
            pltpu.VMEM((2, rows_count, LANES), jnp.float32),
            pltpu.VMEM((own // R, coarse, cols_count), jnp.float32),
        ],
        compiler_params=pltpu.CompilerParams(
            vmem_limit_bytes=18 * 2**20, dimension_semantics=("arbitrary",)
        ),
        cost_estimate=pl.CostEstimate(
            flops=200_000_000, bytes_accessed=34 * 2**20, transcendentals=0
        ),
        name="sweep",
    )(
        source_plane,
        *rates,
        *states,
        velocity,
        profile,
        *fields,
        columns_table,
    )


def exact_dot(a, b):
    return jnp.dot(a, b, precision=lax.Precision.HIGHEST, preferred_element_type=jnp.float32)


def filter_kernel(lam_second, received, table_ref, symbol_depth, symbol_rows, out_ref, field):
    depth_blocks, tracers, planes, size = received.shape
    for block in range(depth_blocks):
        field[block * planes : (block + 1) * planes, :] = jnp.sum(received[block], axis=0)
    table = table_ref[...]
    spectrum = exact_dot(exact_dot(table, field[...]), table)
    lam = symbol_depth[...] + symbol_rows[...] + lam_second[0]
    factor = 1.0 + PRIOR_RANGE * lam
    spectrum = spectrum * (1.0 / (factor * factor) / float(size**3))
    field[...] = exact_dot(exact_dot(table, spectrum), table)
    share = size // tracers
    group = lax.broadcasted_iota(jnp.int32, (depth_blocks, size), 1) // share
    by_plane = [field[pl.ds(plane, depth_blocks, planes), :] for plane in range(planes)]
    for tracer in range(tracers):
        part = jnp.zeros((depth_blocks, size), jnp.float32)
        for plane in range(planes):
            shift = (plane - tracer) * share % size
            moved = pltpu.roll(by_plane[plane], shift, 1) if shift else by_plane[plane]
            part = jnp.where(group == plane, moved, part)
        out_ref[pl.ds(tracer, depth_blocks, tracers), :] = part


def filtered(received, own_symbol):
    depth_blocks, tracers, planes, size = received.shape
    line = symbol(size)
    vmem = pl.BlockSpec(memory_space=pltpu.VMEM)
    return pl.pallas_call(
        filter_kernel,
        out_shape=jax.ShapeDtypeStruct((depth_blocks * tracers, size), jnp.float32),
        in_specs=[pl.BlockSpec(memory_space=pltpu.SMEM)] + [vmem] * 4,
        out_specs=vmem,
        scratch_shapes=[pltpu.VMEM((depth_blocks * planes, size), jnp.float32)],
        compiler_params=pltpu.CompilerParams(vmem_limit_bytes=16 * 2**20),
        name="filter",
    )(
        own_symbol,
        received,
        jnp.asarray(hartley(size)),
        jnp.asarray(line[:, None]),
        jnp.asarray(line[None, :]),
    )


def inverse_kernel(received, table_ref, out_ref):
    out_ref[...] = lax.dot_general(
        received[...],
        table_ref[...],
        (((0,), (0,)), ((), ())),
        precision=lax.Precision.HIGHEST,
        preferred_element_type=jnp.float32,
    )


def inverse_columns(received):
    vmem = pl.BlockSpec(memory_space=pltpu.VMEM)
    return pl.pallas_call(
        inverse_kernel,
        out_shape=jax.ShapeDtypeStruct(received.shape, jnp.float32),
        in_specs=[vmem, vmem],
        out_specs=vmem,
        compiler_params=pltpu.CompilerParams(vmem_limit_bytes=16 * 2**20),
        name="inverse_columns",
    )(received, jnp.asarray(hartley(received.shape[0])))


def neighbours(first, last):
    count = lax.axis_size("domain")
    up = [(i, (i + 1) % count) for i in range(count)]
    down = [(j, i) for i, j in up]
    return lax.ppermute(last, "domain", up), lax.ppermute(first, "domain", down)


def local(log_rate, velocity, initial, profile, plane, depth, row, column, step_of, observed):
    slab, rows_count, cols_count = log_rate.shape
    domain_count, tracer_count = lax.axis_size("domain"), lax.axis_size("tracer")
    full = slab * domain_count
    offset = lax.axis_index("domain") * slab
    low, high = neighbours(
        jnp.stack([log_rate[:HALO], initial[0, :HALO]]),
        jnp.stack([log_rate[-HALO:], initial[0, -HALO:]]),
    )
    keys, values, starts, rate_near, state_near = sort_probes(
        offset.astype(jnp.int32)[None],
        depth,
        row,
        column,
        step_of,
        observed,
        slab + 2 * LEAD,
        log_rate,
        initial[0],
    )
    source_plane = (plane - (offset - HALO)) % full
    fields = bin_probes(starts, keys, values, rows_count, cols_count)
    rates = (low, rate_near, high)
    states = (low, state_near, high)
    spectral = sweep(source_plane, rates, states, velocity, profile, fields)
    first, planes, second = rows_count // R, slab // R, cols_count // R
    axes = ("domain", "tracer")
    received = lax.all_to_all(
        spectral.reshape(second, planes, first), axes, split_axis=0, concat_axis=0, tiled=True
    )
    own = lax.axis_index("domain") * tracer_count + lax.axis_index("tracer")
    own_symbol = lax.dynamic_slice(jnp.asarray(symbol(second)), (own,), (1,))
    back = filtered(received.reshape(domain_count, tracer_count, planes, first), own_symbol)
    result = lax.all_to_all(back, axes, split_axis=0, concat_axis=0, tiled=True)
    return inverse_columns(result).reshape(planes, first // tracer_count, second)


def solution(mesh):
    return jax.shard_map(
        local,
        mesh=mesh,
        in_specs=(
            P("domain", None, None),
            P(),
            P("tracer", "domain", None, None),
            P("tracer", None, None),
            P("tracer"),
            P("tracer", None),
            P("tracer", None),
            P("tracer", None),
            P("tracer", None),
            P("tracer", None),
        ),
        out_specs=P("domain", "tracer", None),
        check_vma=False,
    )
```

```python
import functools
import math

import jax
import jax.numpy as jnp
import numpy as np
from jax import lax
from jax.experimental import pallas as pl
from jax.experimental.pallas import tpu as pltpu
from jax.sharding import PartitionSpec as P

R = 2
STEPS = 2
TIME_STEP = 0.14
PRIOR_RANGE = 4.0

HALO = 4
LEAD = 2
LANES = 128
LONG, SHORT = 8, 4
PAD = 8
STRIP = 32


def hartley(length):
    phases = np.outer(np.arange(length), np.arange(length)) % length
    angles = 2.0 * math.pi / length * phases
    return (np.cos(angles) + np.sin(angles)).astype(np.float32)


def symbol(length):
    return (2.0 - 2.0 * np.cos(2.0 * math.pi / length * np.arange(length))).astype(np.float32)


def sort_kernel(
    offset_ref,
    depth_far,
    row_far,
    column_far,
    step_far,
    observed_far,
    rate,
    state,
    keys_out,
    values_out,
    starts_out,
    rate_near,
    state_near,
    keys,
    values,
    depth_ref,
    row_ref,
    column_ref,
    step_ref,
    observed_ref,
    sems,
):
    probes = [
        pltpu.make_async_copy(far, near, sems.at[2 + at])
        for at, (far, near) in enumerate(
            (
                (depth_far, depth_ref),
                (row_far, row_ref),
                (column_far, column_ref),
                (step_far, step_ref),
                (observed_far, observed_ref),
            )
        )
    ]
    for copy in probes:
        copy.start()
    near = [
        pltpu.make_async_copy(rate, rate_near, sems.at[0]),
        pltpu.make_async_copy(state, state_near, sems.at[1]),
    ]
    for copy in near:
        copy.start()
    for copy in probes:
        copy.wait()
    offset = offset_ref[0]
    plane = (depth_ref[...] - (offset - LEAD)) & 255
    key = (plane << 17) | ((step_ref[...] - 1) << 16) | (row_ref[...] << 8) | column_ref[...]
    keys[...] = key.reshape(keys.shape)
    values[...] = observed_ref[...].reshape(values.shape)
    for index in range(starts_out.shape[0]):
        if index == 0:
            starts_out[index] = 0
        else:
            starts_out[index] = jnp.sum((key < (index << 17)).astype(jnp.int32))

    lane = lax.broadcasted_iota(jnp.int32, (8, LANES), 1)
    sublane = lax.broadcasted_iota(jnp.int32, (8, LANES), 0)

    def pair(low, high, down):
        (key_a, value_a), (key_b, value_b) = low, high
        if down is False:
            swap = key_a > key_b
        elif down is True:
            swap = key_a < key_b
        else:
            swap = jnp.logical_xor(key_a > key_b, down)
        return (
            (jnp.where(swap, key_b, key_a), jnp.where(swap, value_b, value_a)),
            (jnp.where(swap, key_a, key_b), jnp.where(swap, value_a, value_b)),
        )

    def within(item, axis, distance, upper, largest):
        key, value = item
        size = key.shape[axis]
        key_p = jnp.where(
            upper, pltpu.roll(key, distance, axis), pltpu.roll(key, size - distance, axis)
        )
        value_p = jnp.where(
            upper, pltpu.roll(value, distance, axis), pltpu.roll(value, size - distance, axis)
        )
        gap = key_p - key
        take = jnp.where(largest, gap, -gap) > 0
        return jnp.where(take, key_p, key), jnp.where(take, value_p, value)

    def bit_of(array, bit):
        return ((array >> bit) & 1) == 1

    def registers(items, level, down):
        for bit in range(level, -1, -1):
            for low in range(16):
                if low & (1 << bit):
                    continue
                high = low | (1 << bit)
                order = down(low) if callable(down) else down
                items[low], items[high] = pair(items[low], items[high], order)
        return items

    def sublanes(items, bit, down):
        upper = bit_of(sublane, bit)
        largest = jnp.logical_xor(upper, down) if not isinstance(down, bool) else (
            jnp.logical_not(upper) if down else upper
        )
        return [within(item, 0, 1 << bit, upper, largest) for item in items]

    def load(group):
        return [(keys[group * 16 + i], values[group * 16 + i]) for i in range(16)]

    def store(group, items):
        for i, (key, value) in enumerate(items):
            keys[group * 16 + i] = key
            values[group * 16 + i] = value

    for group in range(2):
        items = load(group)
        for level in range(1, 4):
            items = registers(
                items, level - 1, lambda low, level=level: bool((low >> level) & 1)
            )
        items = registers(items, 3, bit_of(sublane, 0))
        for level in range(1, 3):
            down = bit_of(sublane, level)
            for bit in range(level - 1, -1, -1):
                items = sublanes(items, bit, down)
            items = registers(items, 3, down)
        down = bool(group)
        for bit in range(2, -1, -1):
            items = sublanes(items, bit, down)
        items = registers(items, 3, down)
        store(group, items)

    def merge(level, carry):
        down = ((lane >> level) & 1) == 1

        def across(turn, inner):
            bit = level - 1 - turn
            distance = jnp.int32(1) << bit
            upper = ((lane >> bit) & 1) == 1
            largest = jnp.logical_xor(upper, down)
            for i in range(32):
                keys[i], values[i] = within((keys[i], values[i]), 1, distance, upper, largest)
            return inner

        lax.fori_loop(0, level, across, 0)
        for i in range(16):
            low, high = pair((keys[i], values[i]), (keys[i + 16], values[i + 16]), down)
            keys[i], values[i] = low
            keys[i + 16], values[i + 16] = high
        for group in range(2):
            items = load(group)
            for bit in range(2, -1, -1):
                items = sublanes(items, bit, down)
            items = registers(items, 3, down)
            store(group, items)
        return carry

    lax.fori_loop(0, 8, merge, 0)

    for half in range(2):
        part = keys[pl.ds(half * 16, 16)].reshape(LANES, LANES)
        keys_out[pl.ds(half, LANES, 2), :] = part.T
        part = values[pl.ds(half * 16, 16)].reshape(LANES, LANES)
        values_out[pl.ds(half, LANES, 2), :] = part.T
    keys_out[2 * LANES :, :] = jnp.full((8, LANES), -1, jnp.int32)
    values_out[2 * LANES :, :] = jnp.zeros((8, LANES), jnp.float32)
    for copy in near:
        copy.wait()


def sort_probes(offset, depth, row, column, step_of, observed, planes, rate, state):
    count = depth.size
    shape = (count // LANES, LANES)
    vmem = pl.BlockSpec(memory_space=pltpu.VMEM)
    smem = pl.BlockSpec(memory_space=pltpu.SMEM)
    stay = pl.BlockSpec(memory_space=pl.ANY)
    return pl.pallas_call(
        sort_kernel,
        out_shape=(
            jax.ShapeDtypeStruct((shape[0] + 8, LANES), jnp.int32),
            jax.ShapeDtypeStruct((shape[0] + 8, LANES), jnp.float32),
            jax.ShapeDtypeStruct((planes + 1,), jnp.int32),
            jax.ShapeDtypeStruct(rate.shape, jnp.float32),
            jax.ShapeDtypeStruct(state.shape, jnp.float32),
        ),
        in_specs=[smem] + [stay] * 7,
        out_specs=(vmem, vmem, smem, stay, stay),
        scratch_shapes=[
            pltpu.VMEM((shape[0] // 8, 8, LANES), jnp.int32),
            pltpu.VMEM((shape[0] // 8, 8, LANES), jnp.float32),
            *[pltpu.VMEM(shape, jnp.int32)] * 4,
            pltpu.VMEM(shape, jnp.float32),
            pltpu.SemaphoreType.DMA((7,)),
        ],
        compiler_params=pltpu.CompilerParams(vmem_limit_bytes=42 * 2**20),
        cost_estimate=pl.CostEstimate(flops=20_000_000, bytes_accessed=2**20, transcendentals=0),
        name="sort_probes",
    )(offset, *(a.reshape(shape) for a in (depth, row, column, step_of, observed)), rate, state)


def bin_kernel(starts, keys_ref, values_ref, *fields):
    place = pl.program_id(0)
    size = fields[0].shape[1]
    both = STEPS * size
    counts, sums = fields[:STEPS], fields[STEPS:]
    begin, end = starts[place], starts[place + 1]
    first = begin >> 7
    windows = (end - (first << 7) + 2 * LANES - 1) >> 8

    def window(turn):
        at = first + 2 * turn
        key = jnp.concatenate([keys_ref[pl.ds(at, 1), :], keys_ref[pl.ds(at + 1, 1), :]], axis=1)
        value = jnp.concatenate(
            [values_ref[pl.ds(at, 1), :], values_ref[pl.ds(at + 1, 1), :]], axis=1
        )
        target = lax.broadcasted_iota(jnp.int32, (both, 2 * LANES), 0) + (place << 9)
        in_row = jnp.where((key >> 8) == target, 1.0, 0.0).astype(jnp.bfloat16)
        in_column = (key & 255) == lax.broadcasted_iota(jnp.int32, (size, 2 * LANES), 0)
        coarse = value.astype(jnp.bfloat16).astype(jnp.float32)
        rest = value - coarse

        def product(amount):
            return lax.dot_general(
                in_row,
                jnp.where(in_column, amount, 0.0).astype(jnp.bfloat16),
                (((1,), (1,)), ((), ())),
                preferred_element_type=jnp.float32,
            )

        return product(1.0), product(coarse) + product(rest)

    def parts(pair):
        for fields_of, values in zip((counts, sums), pair):
            for step, field in enumerate(fields_of):
                yield field, values[step * size : (step + 1) * size]

    for field, value in parts(window(0)):
        field[0] = value

    def more(turn, carry):
        for field, value in parts(window(turn)):
            field[0] += value
        return carry

    lax.fori_loop(1, windows, more, 0)


def bin_probes(starts, keys, values, rows_count, cols_count):
    places = starts.shape[0] - 1
    vmem = pl.BlockSpec(memory_space=pltpu.VMEM)
    block = pl.BlockSpec((1, rows_count, cols_count), lambda i: (i, 0, 0))
    field = jax.ShapeDtypeStruct((places, rows_count, cols_count), jnp.float32)
    return pl.pallas_call(
        bin_kernel,
        grid=(places,),
        out_shape=(field,) * (2 * STEPS),
        in_specs=[pl.BlockSpec(memory_space=pltpu.SMEM), vmem, vmem],
        out_specs=(block,) * (2 * STEPS),
        compiler_params=pltpu.CompilerParams(
            vmem_limit_bytes=5 * 2**20, dimension_semantics=("arbitrary",)
        ),
        cost_estimate=pl.CostEstimate(
            flops=30_000_000, bytes_accessed=20 * 2**20, transcendentals=0
        ),
        name="bin_probes",
    )(starts, keys, values)


def ahead(parts):
    lane = lax.broadcasted_iota(jnp.int32, parts[0].shape, 1)
    left, right = (pltpu.roll(part, LANES - 1, 1) for part in parts)
    last = lane == LANES - 1
    return jnp.where(last, right, left), jnp.where(last, left, right)


def behind(parts):
    lane = lax.broadcasted_iota(jnp.int32, parts[0].shape, 1)
    left, right = (pltpu.roll(part, 1, 1) for part in parts)
    first = lane == 0
    return jnp.where(first, right, left), jnp.where(first, left, right)


def sweep_kernel(
    source_plane,
    rate_low,
    rate_own,
    rate_high,
    state_low,
    state_own,
    state_high,
    velocity_ref,
    profile_ref,
    count1,
    count2,
    sum1,
    sum2,
    columns_table,
    out_ref,
    half_rate,
    state0,
    state1,
    adjoint2,
    adjoint1,
    face_x,
    grad_x0,
    grad_x1,
    grad_x2,
    inject1,
    depth_product,
    pair_sum,
    coarse_rows,
):
    index = pl.program_id(0)
    total = pl.num_programs(0)
    size = half_rate.shape[2] - 2 * PAD
    halves = range(2)
    strips = range(0, size, STRIP)

    def rows(ref, plane, half, start, shift=0):
        slot = plane & (ref.shape[0] - 1)
        return ref[slot, half, PAD + start + shift : PAD + start + shift + STRIP, :]

    def put(ref, plane, half, start, value):
        slot = plane & (ref.shape[0] - 1)
        ref[slot, half, PAD + start : PAD + start + STRIP, :] = value
        if start == 0:
            ref[slot, half, PAD + size : PAD + size + 1, :] = value[:1]
        if start + STRIP == size:
            ref[slot, half, PAD - 1 : PAD, :] = value[STRIP - 1 :]

    def plain(ref, plane, half, start):
        return ref[plane & (ref.shape[0] - 1), half, start : start + STRIP, :]

    def put_plain(ref, plane, half, start, value):
        ref[plane & (ref.shape[0] - 1), half, start : start + STRIP, :] = value

    def enter(rate_ref, state_ref):
        for start in strips:
            span = slice(start, start + STRIP)
            rate, state = [], []
            for half in halves:
                cols = slice(half * LANES, (half + 1) * LANES)
                rate.append((0.5 * TIME_STEP) * jnp.exp(rate_ref[0, span, cols]))
                state.append(state_ref[0, span, cols])
            rate_ahead, state_ahead = ahead(rate), ahead(state)
            for half in halves:
                put(half_rate, index, half, start, rate[half])
                put(state0, index, half, start, state[half])
                put_plain(face_x, index, half, start, rate[half] + rate_ahead[half])
                put_plain(grad_x0, index, half, start, state_ahead[half] - state[half])

    @pl.when(index < HALO)
    def _():
        enter(rate_low, state_low)

    @pl.when((index >= HALO) & (index < total - HALO))
    def _():
        enter(rate_own, state_own)

    @pl.when((index >= total - HALO) & (index < total))
    def _():
        enter(rate_high, state_high)

    def advance(field, grad_x, slot, start, adjoint):
        up, down = slot + 1, slot - 1
        flux = [
            plain(face_x, slot, half, start) * plain(grad_x, slot, half, start) for half in halves
        ]
        flux_behind = behind(flux)
        result = []
        for half in halves:
            value = rows(field, slot, half, start)
            rate = rows(half_rate, slot, half, start)
            wind = TIME_STEP * velocity_ref[
                start : start + STRIP, half * LANES : (half + 1) * LANES
            ]
            rate_up = rate + rows(half_rate, up, half, start)
            rate_down = rate + rows(half_rate, down, half, start)
            if adjoint:
                rate_up = rate_up + wind
            else:
                rate_down = rate_down + wind
            depth_part = rate_up * (rows(field, up, half, start) - value) - rate_down * (
                value - rows(field, down, half, start)
            )
            row_part = (rate + rows(half_rate, slot, half, start, 1)) * (
                rows(field, slot, half, start, 1) - value
            ) - (rate + rows(half_rate, slot, half, start, -1)) * (
                value - rows(field, slot, half, start, -1)
            )
            result.append(value + depth_part + row_part + (flux[half] - flux_behind[half]))
        return result

    def save(field, grad_x, slot, start, parts):
        parts_ahead = ahead(parts)
        for half in halves:
            put(field, slot, half, start, parts[half])
            put_plain(grad_x, slot, half, start, parts_ahead[half] - parts[half])

    def source_gain(plane):
        return jnp.where(plane == source_plane[0], jnp.float32(TIME_STEP), jnp.float32(0.0))

    def source(gain, half, start):
        return gain * profile_ref[0, start : start + STRIP, half * LANES : (half + 1) * LANES]

    plane1 = index - 1

    @pl.when((plane1 >= 1) & (plane1 < total - 1))
    def _():
        slot = plane1
        gain = source_gain(plane1)
        for start in strips:
            parts = advance(state0, grad_x0, slot, start, False)
            parts = [parts[half] + source(gain, half, start) for half in halves]
            save(state1, grad_x1, slot, start, parts)

    plane2 = index - 2

    @pl.when((plane2 >= 2) & (plane2 < total - 2))
    def _():
        slot = plane2
        gain = source_gain(plane2)
        for start in strips:
            parts = advance(state1, grad_x1, slot, start, False)
            mu = []
            for half in halves:
                cols = slice(half * LANES, (half + 1) * LANES)
                state2 = parts[half] + source(gain, half, start)
                span = slice(start, start + STRIP)
                mu.append(count2[0, span, cols] * state2 - sum2[0, span, cols])
                put_plain(
                    inject1,
                    slot,
                    half,
                    start,
                    count1[0, span, cols] * rows(state1, slot, half, start) - sum1[0, span, cols],
                )
            save(adjoint2, grad_x2, slot, start, mu)

    plane3 = index - 3

    @pl.when((plane3 >= 3) & (plane3 < total - 3))
    def _():
        slot = plane3
        for start in strips:
            parts = advance(adjoint2, grad_x2, slot, start, True)
            for half in halves:
                put(
                    adjoint1,
                    slot,
                    half,
                    start,
                    parts[half] + plain(inject1, slot, half, start),
                )

    plane4 = index - 4

    def products(slot, other, half, start):
        def step(field):
            return rows(field, other, half, start) - rows(field, slot, half, start)

        return step(state0) * step(adjoint1) + step(state1) * step(adjoint2)

    @pl.when(plane4 == HALO - 1)
    def _():
        slot = plane4
        for start in strips:
            for half in halves:
                depth_product[half, start : start + STRIP, :] = products(
                    slot, slot + 1, half, start
                )

    @pl.when(plane4 >= HALO)
    def _():
        slot, up = plane4, plane4 + 1
        even = (plane4 & 1) == 0
        for start in strips:
            mu = [rows(adjoint1, slot, half, start) for half in halves]
            mu_ahead = ahead(mu)
            product_x = [
                plain(grad_x0, slot, half, start) * (mu_ahead[half] - mu[half])
                + plain(grad_x1, slot, half, start) * plain(grad_x2, slot, half, start)
                for half in halves
            ]
            product_behind = behind(product_x)
            for half in halves:
                span = slice(start, start + STRIP)
                result = product_x[half] + product_behind[half]
                upper = products(slot, up, half, start)
                result = result + (upper + depth_product[half, span, :])
                depth_product[half, span, :] = upper
                for shift in (1, -1):
                    factors = [
                        rows(field, slot, half, start, shift) - rows(field, slot, half, start)
                        for field in (state0, adjoint1, state1, adjoint2)
                    ]
                    result = result + (factors[0] * factors[1] + factors[2] * factors[3])
                result = -rows(half_rate, slot, half, start) * result
                pair_sum[half, span, :] = jnp.where(even, 0.0, pair_sum[half, span, :]) + result

    @pl.when((plane4 >= HALO) & ((plane4 & 1) == 1))
    def _():
        for half in halves:
            even_rows = pair_sum[half, pl.ds(0, size // R, R), :]
            odd_rows = pair_sum[half, pl.ds(1, size // R, R), :]
            cols = slice(half * LANES, (half + 1) * LANES)
            coarse_rows[(plane4 - HALO) >> 1, :, cols] = even_rows + odd_rows

    @pl.when(index == total - 1)
    def _():
        planes = coarse_rows.shape[0]
        for plane in range(planes):
            out_ref[pl.ds(plane, columns_table.shape[0], planes), :] = lax.dot_general(
                columns_table[...],
                coarse_rows[plane],
                (((1,), (1,)), ((), ())),
                precision=lax.Precision.HIGHEST,
                preferred_element_type=jnp.float32,
            )


def sweep(source_plane, rates, states, velocity, profile, fields):
    own, rows_count, cols_count = rates[1].shape
    total = own + 2 * HALO
    coarse = rows_count // R
    plane = (1, rows_count, cols_count)
    smem = pl.BlockSpec(memory_space=pltpu.SMEM)
    vmem = pl.BlockSpec(memory_space=pltpu.VMEM)

    def low(which):
        return pl.BlockSpec((None, *plane), lambda i: (which, jnp.minimum(i, HALO - 1), 0, 0))

    def high(which):
        return pl.BlockSpec(
            (None, *plane), lambda i: (which, jnp.clip(i - HALO - own, 0, HALO - 1), 0, 0)
        )

    middle = pl.BlockSpec(plane, lambda i: (jnp.clip(i - HALO, 0, own - 1), 0, 0))
    columns_table = jnp.asarray(np.repeat(hartley(cols_count // R), R, axis=1))
    voxels = pl.BlockSpec(
        (1, rows_count, cols_count),
        lambda i: (jnp.clip(i - HALO, 0, total - 2 * LEAD - 1), 0, 0),
    )
    def padded(kept):
        return pltpu.VMEM((kept, 2, rows_count + 2 * PAD, LANES), jnp.float32)

    def plain(kept):
        return pltpu.VMEM((kept, 2, rows_count, LANES), jnp.float32)

    return pl.pallas_call(
        sweep_kernel,
        grid=(total,),
        out_shape=jax.ShapeDtypeStruct((cols_count // R * (own // R), coarse), jnp.float32),
        in_specs=[smem, low(0), middle, high(0), low(1), middle, high(1), vmem, vmem] + [voxels] * 4 + [vmem],
        out_specs=vmem,
        scratch_shapes=[padded(LONG)] * 2
        + [padded(SHORT)] * 3
        + [plain(SHORT), plain(LONG), plain(SHORT), plain(SHORT), plain(2)]
        + [
            pltpu.VMEM((2, rows_count, LANES), jnp.float32),
            pltpu.VMEM((2, rows_count, LANES), jnp.float32),
            pltpu.VMEM((own // R, coarse, cols_count), jnp.float32),
        ],
        compiler_params=pltpu.CompilerParams(
            vmem_limit_bytes=18 * 2**20, dimension_semantics=("arbitrary",)
        ),
        cost_estimate=pl.CostEstimate(
            flops=200_000_000, bytes_accessed=34 * 2**20, transcendentals=0
        ),
        name="sweep",
    )(
        source_plane,
        *rates,
        *states,
        velocity,
        profile,
        *fields,
        columns_table,
    )


def exact_dot(a, b):
    return jnp.dot(a, b, precision=lax.Precision.HIGHEST, preferred_element_type=jnp.float32)


def filter_kernel(lam_second, received, table_ref, symbol_depth, symbol_rows, out_ref, field):
    depth_blocks, tracers, planes, size = received.shape
    for block in range(depth_blocks):
        field[block * planes : (block + 1) * planes, :] = jnp.sum(received[block], axis=0)
    table = table_ref[...]
    spectrum = exact_dot(exact_dot(table, field[...]), table)
    lam = symbol_depth[...] + symbol_rows[...] + lam_second[0]
    factor = 1.0 + PRIOR_RANGE * lam
    spectrum = spectrum * (1.0 / (factor * factor) / float(size**3))
    field[...] = exact_dot(exact_dot(table, spectrum), table)
    share = size // tracers
    group = lax.broadcasted_iota(jnp.int32, (depth_blocks, size), 1) // share
    by_plane = [field[pl.ds(plane, depth_blocks, planes), :] for plane in range(planes)]
    for tracer in range(tracers):
        part = jnp.zeros((depth_blocks, size), jnp.float32)
        for plane in range(planes):
            shift = (plane - tracer) * share % size
            moved = pltpu.roll(by_plane[plane], shift, 1) if shift else by_plane[plane]
            part = jnp.where(group == plane, moved, part)
        out_ref[pl.ds(tracer, depth_blocks, tracers), :] = part


def filtered(received, own_symbol):
    depth_blocks, tracers, planes, size = received.shape
    line = symbol(size)
    vmem = pl.BlockSpec(memory_space=pltpu.VMEM)
    return pl.pallas_call(
        filter_kernel,
        out_shape=jax.ShapeDtypeStruct((depth_blocks * tracers, size), jnp.float32),
        in_specs=[pl.BlockSpec(memory_space=pltpu.SMEM)] + [vmem] * 4,
        out_specs=vmem,
        scratch_shapes=[pltpu.VMEM((depth_blocks * planes, size), jnp.float32)],
        compiler_params=pltpu.CompilerParams(vmem_limit_bytes=16 * 2**20),
        name="filter",
    )(
        own_symbol,
        received,
        jnp.asarray(hartley(size)),
        jnp.asarray(line[:, None]),
        jnp.asarray(line[None, :]),
    )


def inverse_kernel(received, table_ref, out_ref):
    out_ref[...] = lax.dot_general(
        received[...],
        table_ref[...],
        (((0,), (0,)), ((), ())),
        precision=lax.Precision.HIGHEST,
        preferred_element_type=jnp.float32,
    )


def inverse_columns(received):
    vmem = pl.BlockSpec(memory_space=pltpu.VMEM)
    return pl.pallas_call(
        inverse_kernel,
        out_shape=jax.ShapeDtypeStruct(received.shape, jnp.float32),
        in_specs=[vmem, vmem],
        out_specs=vmem,
        compiler_params=pltpu.CompilerParams(vmem_limit_bytes=16 * 2**20),
        name="inverse_columns",
    )(received, jnp.asarray(hartley(received.shape[0])))


def edges_kernel(rate, state, first, last, sems):
    begin = rate.shape[0] - HALO
    copies = [
        pltpu.make_async_copy(source.at[pl.ds(at, HALO)], target.at[which], sems.at[which, side])
        for which, source in enumerate((rate, state))
        for side, (at, target) in enumerate(((0, first), (begin, last)))
    ]
    for copy in copies:
        copy.start()
    for copy in copies:
        copy.wait()


def edges(rate, state):
    stay = pl.BlockSpec(memory_space=pl.ANY)
    vmem = pl.BlockSpec(memory_space=pltpu.VMEM)
    end = jax.ShapeDtypeStruct((2, HALO, *rate.shape[1:]), jnp.float32)
    return pl.pallas_call(
        edges_kernel,
        out_shape=(end, end),
        in_specs=[stay, stay],
        out_specs=(vmem, vmem),
        scratch_shapes=[pltpu.SemaphoreType.DMA((2, 2))],
        compiler_params=pltpu.CompilerParams(vmem_limit_bytes=50 * 2**20),
        name="edges",
    )(rate, state)


def neighbours(first, last):
    count = lax.axis_size("domain")
    up = [(i, (i + 1) % count) for i in range(count)]
    down = [(j, i) for i, j in up]
    return lax.ppermute(last, "domain", up), lax.ppermute(first, "domain", down)


def local(log_rate, velocity, initial, profile, plane, depth, row, column, step_of, observed):
    slab, rows_count, cols_count = log_rate.shape
    domain_count, tracer_count = lax.axis_size("domain"), lax.axis_size("tracer")
    full = slab * domain_count
    offset = lax.axis_index("domain") * slab
    low, high = neighbours(*edges(log_rate, initial[0]))
    keys, values, starts, rate_near, state_near = sort_probes(
        offset.astype(jnp.int32)[None],
        depth,
        row,
        column,
        step_of,
        observed,
        slab + 2 * LEAD,
        log_rate,
        initial[0],
    )
    source_plane = (plane - (offset - HALO)) % full
    fields = bin_probes(starts, keys, values, rows_count, cols_count)
    rates = (low, rate_near, high)
    states = (low, state_near, high)
    spectral = sweep(source_plane, rates, states, velocity, profile, fields)
    first, planes, second = rows_count // R, slab // R, cols_count // R
    axes = ("domain", "tracer")
    received = lax.all_to_all(
        spectral.reshape(second, planes, first), axes, split_axis=0, concat_axis=0, tiled=True
    )
    own = lax.axis_index("domain") * tracer_count + lax.axis_index("tracer")
    own_symbol = lax.dynamic_slice(jnp.asarray(symbol(second)), (own,), (1,))
    back = filtered(received.reshape(domain_count, tracer_count, planes, first), own_symbol)
    result = lax.all_to_all(back, axes, split_axis=0, concat_axis=0, tiled=True)
    return inverse_columns(result).reshape(planes, first // tracer_count, second)


def solution(mesh):
    return jax.shard_map(
        local,
        mesh=mesh,
        in_specs=(
            P("domain", None, None),
            P(),
            P("tracer", "domain", None, None),
            P("tracer", None, None),
            P("tracer"),
            P("tracer", None),
            P("tracer", None),
            P("tracer", None),
            P("tracer", None),
            P("tracer", None),
        ),
        out_specs=P("domain", "tracer", None),
        check_vma=False,
    )
```

```python
import functools
import math

import jax
import jax.numpy as jnp
import numpy as np
from jax import lax
from jax.experimental import pallas as pl
from jax.experimental.pallas import tpu as pltpu
from jax.sharding import PartitionSpec as P

R = 2
STEPS = 2
TIME_STEP = 0.14
PRIOR_RANGE = 4.0

HALO = 4
LEAD = 2
LANES = 128
LONG, SHORT = 8, 4
PAD = 8
STRIP = 32


def hartley(length):
    phases = np.outer(np.arange(length), np.arange(length)) % length
    angles = 2.0 * math.pi / length * phases
    return (np.cos(angles) + np.sin(angles)).astype(np.float32)


def symbol(length):
    return (2.0 - 2.0 * np.cos(2.0 * math.pi / length * np.arange(length))).astype(np.float32)


def sort_kernel(
    offset_ref,
    depth_far,
    row_far,
    column_far,
    step_far,
    observed_far,
    rate,
    state,
    keys_out,
    values_out,
    starts_out,
    rate_near,
    state_near,
    keys,
    values,
    depth_ref,
    row_ref,
    column_ref,
    step_ref,
    observed_ref,
    sems,
):
    probes = [
        pltpu.make_async_copy(far, near, sems.at[2 + at])
        for at, (far, near) in enumerate(
            (
                (depth_far, depth_ref),
                (row_far, row_ref),
                (column_far, column_ref),
                (step_far, step_ref),
                (observed_far, observed_ref),
            )
        )
    ]
    for copy in probes:
        copy.start()
    near = [
        pltpu.make_async_copy(rate, rate_near, sems.at[0]),
        pltpu.make_async_copy(state, state_near, sems.at[1]),
    ]
    for copy in near:
        copy.start()
    for copy in probes:
        copy.wait()
    offset = offset_ref[0]
    plane = (depth_ref[...] - (offset - LEAD)) & 255
    key = (plane << 17) | ((step_ref[...] - 1) << 16) | (row_ref[...] << 8) | column_ref[...]
    keys[...] = key.reshape(keys.shape)
    values[...] = observed_ref[...].reshape(values.shape)
    for index in range(starts_out.shape[0]):
        if index == 0:
            starts_out[index] = 0
        else:
            starts_out[index] = jnp.sum((key < (index << 17)).astype(jnp.int32))

    lane = lax.broadcasted_iota(jnp.int32, (8, LANES), 1)
    sublane = lax.broadcasted_iota(jnp.int32, (8, LANES), 0)

    def pair(low, high, down):
        (key_a, value_a), (key_b, value_b) = low, high
        if down is False:
            swap = key_a > key_b
        elif down is True:
            swap = key_a < key_b
        else:
            swap = jnp.logical_xor(key_a > key_b, down)
        return (
            (jnp.where(swap, key_b, key_a), jnp.where(swap, value_b, value_a)),
            (jnp.where(swap, key_a, key_b), jnp.where(swap, value_a, value_b)),
        )

    def within(item, axis, distance, upper, largest):
        key, value = item
        size = key.shape[axis]
        key_p = jnp.where(
            upper, pltpu.roll(key, distance, axis), pltpu.roll(key, size - distance, axis)
        )
        value_p = jnp.where(
            upper, pltpu.roll(value, distance, axis), pltpu.roll(value, size - distance, axis)
        )
        gap = key_p - key
        take = jnp.where(largest, gap, -gap) > 0
        return jnp.where(take, key_p, key), jnp.where(take, value_p, value)

    def bit_of(array, bit):
        return ((array >> bit) & 1) == 1

    def registers(items, level, down):
        for bit in range(level, -1, -1):
            for low in range(16):
                if low & (1 << bit):
                    continue
                high = low | (1 << bit)
                order = down(low) if callable(down) else down
                items[low], items[high] = pair(items[low], items[high], order)
        return items

    def sublanes(items, bit, down):
        upper = bit_of(sublane, bit)
        largest = jnp.logical_xor(upper, down) if not isinstance(down, bool) else (
            jnp.logical_not(upper) if down else upper
        )
        return [within(item, 0, 1 << bit, upper, largest) for item in items]

    def load(group):
        return [(keys[group * 16 + i], values[group * 16 + i]) for i in range(16)]

    def store(group, items):
        for i, (key, value) in enumerate(items):
            keys[group * 16 + i] = key
            values[group * 16 + i] = value

    for group in range(2):
        items = load(group)
        for level in range(1, 4):
            items = registers(
                items, level - 1, lambda low, level=level: bool((low >> level) & 1)
            )
        items = registers(items, 3, bit_of(sublane, 0))
        for level in range(1, 3):
            down = bit_of(sublane, level)
            for bit in range(level - 1, -1, -1):
                items = sublanes(items, bit, down)
            items = registers(items, 3, down)
        down = bool(group)
        for bit in range(2, -1, -1):
            items = sublanes(items, bit, down)
        items = registers(items, 3, down)
        store(group, items)

    def merge(level, carry):
        down = ((lane >> level) & 1) == 1

        def across(turn, inner):
            bit = level - 1 - turn
            distance = jnp.int32(1) << bit
            upper = ((lane >> bit) & 1) == 1
            largest = jnp.logical_xor(upper, down)
            for i in range(32):
                keys[i], values[i] = within((keys[i], values[i]), 1, distance, upper, largest)
            return inner

        lax.fori_loop(0, level, across, 0)
        for i in range(16):
            low, high = pair((keys[i], values[i]), (keys[i + 16], values[i + 16]), down)
            keys[i], values[i] = low
            keys[i + 16], values[i + 16] = high
        for group in range(2):
            items = load(group)
            for bit in range(2, -1, -1):
                items = sublanes(items, bit, down)
            items = registers(items, 3, down)
            store(group, items)
        return carry

    lax.fori_loop(0, 8, merge, 0)

    for half in range(2):
        part = keys[pl.ds(half * 16, 16)].reshape(LANES, LANES)
        keys_out[pl.ds(half, LANES, 2), :] = part.T
        part = values[pl.ds(half * 16, 16)].reshape(LANES, LANES)
        values_out[pl.ds(half, LANES, 2), :] = part.T
    keys_out[2 * LANES :, :] = jnp.full((8, LANES), -1, jnp.int32)
    values_out[2 * LANES :, :] = jnp.zeros((8, LANES), jnp.float32)
    for copy in near:
        copy.wait()


def sort_probes(offset, depth, row, column, step_of, observed, planes, rate, state):
    count = depth.size
    shape = (count // LANES, LANES)
    vmem = pl.BlockSpec(memory_space=pltpu.VMEM)
    smem = pl.BlockSpec(memory_space=pltpu.SMEM)
    stay = pl.BlockSpec(memory_space=pl.ANY)
    return pl.pallas_call(
        sort_kernel,
        out_shape=(
            jax.ShapeDtypeStruct((shape[0] + 8, LANES), jnp.int32),
            jax.ShapeDtypeStruct((shape[0] + 8, LANES), jnp.float32),
            jax.ShapeDtypeStruct((planes + 1,), jnp.int32),
            jax.ShapeDtypeStruct(rate.shape, jnp.float32),
            jax.ShapeDtypeStruct(state.shape, jnp.float32),
        ),
        in_specs=[smem] + [stay] * 7,
        out_specs=(vmem, vmem, smem, stay, stay),
        scratch_shapes=[
            pltpu.VMEM((shape[0] // 8, 8, LANES), jnp.int32),
            pltpu.VMEM((shape[0] // 8, 8, LANES), jnp.float32),
            *[pltpu.VMEM(shape, jnp.int32)] * 4,
            pltpu.VMEM(shape, jnp.float32),
            pltpu.SemaphoreType.DMA((7,)),
        ],
        compiler_params=pltpu.CompilerParams(vmem_limit_bytes=42 * 2**20),
        cost_estimate=pl.CostEstimate(flops=20_000_000, bytes_accessed=2**20, transcendentals=0),
        name="sort_probes",
    )(offset, *(a.reshape(shape) for a in (depth, row, column, step_of, observed)), rate, state)


def bin_kernel(starts, keys_ref, values_ref, *fields):
    place = pl.program_id(0)
    size = fields[0].shape[1]
    both = STEPS * size
    counts, sums = fields[:STEPS], fields[STEPS:]
    begin, end = starts[place], starts[place + 1]
    first = begin >> 7
    windows = (end - (first << 7) + 2 * LANES - 1) >> 8

    def window(turn):
        at = first + 2 * turn
        key = jnp.concatenate([keys_ref[pl.ds(at, 1), :], keys_ref[pl.ds(at + 1, 1), :]], axis=1)
        value = jnp.concatenate(
            [values_ref[pl.ds(at, 1), :], values_ref[pl.ds(at + 1, 1), :]], axis=1
        )
        target = lax.broadcasted_iota(jnp.int32, (both, 2 * LANES), 0) + (place << 9)
        in_row = jnp.where((key >> 8) == target, 1.0, 0.0).astype(jnp.bfloat16)
        in_column = (key & 255) == lax.broadcasted_iota(jnp.int32, (size, 2 * LANES), 0)
        coarse = value.astype(jnp.bfloat16).astype(jnp.float32)
        rest = value - coarse

        def product(amount):
            return lax.dot_general(
                in_row,
                jnp.where(in_column, amount, 0.0).astype(jnp.bfloat16),
                (((1,), (1,)), ((), ())),
                preferred_element_type=jnp.float32,
            )

        return product(1.0), product(coarse) + product(rest)

    def parts(pair):
        for fields_of, values in zip((counts, sums), pair):
            for step, field in enumerate(fields_of):
                yield field, values[step * size : (step + 1) * size]

    for field, value in parts(window(0)):
        field[0] = value

    def more(turn, carry):
        for field, value in parts(window(turn)):
            field[0] += value
        return carry

    lax.fori_loop(1, windows, more, 0)


def bin_probes(starts, keys, values, rows_count, cols_count):
    places = starts.shape[0] - 1
    vmem = pl.BlockSpec(memory_space=pltpu.VMEM)
    block = pl.BlockSpec((1, rows_count, cols_count), lambda i: (i, 0, 0))
    field = jax.ShapeDtypeStruct((places, rows_count, cols_count), jnp.float32)
    return pl.pallas_call(
        bin_kernel,
        grid=(places,),
        out_shape=(field,) * (2 * STEPS),
        in_specs=[pl.BlockSpec(memory_space=pltpu.SMEM), vmem, vmem],
        out_specs=(block,) * (2 * STEPS),
        compiler_params=pltpu.CompilerParams(
            vmem_limit_bytes=5 * 2**20, dimension_semantics=("arbitrary",)
        ),
        cost_estimate=pl.CostEstimate(
            flops=30_000_000, bytes_accessed=20 * 2**20, transcendentals=0
        ),
        name="bin_probes",
    )(starts, keys, values)


def ahead(parts):
    lane = lax.broadcasted_iota(jnp.int32, parts[0].shape, 1)
    left, right = (pltpu.roll(part, LANES - 1, 1) for part in parts)
    last = lane == LANES - 1
    return jnp.where(last, right, left), jnp.where(last, left, right)


def behind(parts):
    lane = lax.broadcasted_iota(jnp.int32, parts[0].shape, 1)
    left, right = (pltpu.roll(part, 1, 1) for part in parts)
    first = lane == 0
    return jnp.where(first, right, left), jnp.where(first, left, right)


def sweep_kernel(
    source_plane,
    rate_low,
    rate_own,
    rate_high,
    state_low,
    state_own,
    state_high,
    velocity_ref,
    profile_ref,
    count1,
    count2,
    sum1,
    sum2,
    columns_table,
    out_ref,
    half_rate,
    state0,
    state1,
    adjoint2,
    adjoint1,
    face_x,
    grad_x0,
    grad_x1,
    grad_x2,
    inject1,
    depth_product,
    pair_sum,
    coarse_rows,
):
    index = pl.program_id(0)
    total = pl.num_programs(0)
    size = half_rate.shape[2] - 2 * PAD
    halves = range(2)
    strips = range(0, size, STRIP)

    def rows(ref, plane, half, start, shift=0):
        slot = plane & (ref.shape[0] - 1)
        return ref[slot, half, PAD + start + shift : PAD + start + shift + STRIP, :]

    def put(ref, plane, half, start, value):
        slot = plane & (ref.shape[0] - 1)
        ref[slot, half, PAD + start : PAD + start + STRIP, :] = value
        if start == 0:
            ref[slot, half, PAD + size : PAD + size + 1, :] = value[:1]
        if start + STRIP == size:
            ref[slot, half, PAD - 1 : PAD, :] = value[STRIP - 1 :]

    def plain(ref, plane, half, start):
        return ref[plane & (ref.shape[0] - 1), half, start : start + STRIP, :]

    def put_plain(ref, plane, half, start, value):
        ref[plane & (ref.shape[0] - 1), half, start : start + STRIP, :] = value

    def enter(rate_ref, state_ref):
        for start in strips:
            span = slice(start, start + STRIP)
            rate, state = [], []
            for half in halves:
                cols = slice(half * LANES, (half + 1) * LANES)
                rate.append((0.5 * TIME_STEP) * jnp.exp(rate_ref[0, span, cols]))
                state.append(state_ref[0, span, cols])
            rate_ahead, state_ahead = ahead(rate), ahead(state)
            for half in halves:
                put(half_rate, index, half, start, rate[half])
                put(state0, index, half, start, state[half])
                put_plain(face_x, index, half, start, rate[half] + rate_ahead[half])
                put_plain(grad_x0, index, half, start, state_ahead[half] - state[half])

    @pl.when(index < HALO)
    def _():
        enter(rate_low, state_low)

    @pl.when((index >= HALO) & (index < total - HALO))
    def _():
        enter(rate_own, state_own)

    @pl.when((index >= total - HALO) & (index < total))
    def _():
        enter(rate_high, state_high)

    def advance(field, grad_x, slot, start, adjoint):
        up, down = slot + 1, slot - 1
        flux = [
            plain(face_x, slot, half, start) * plain(grad_x, slot, half, start) for half in halves
        ]
        flux_behind = behind(flux)
        result = []
        for half in halves:
            value = rows(field, slot, half, start)
            rate = rows(half_rate, slot, half, start)
            wind = TIME_STEP * velocity_ref[
                start : start + STRIP, half * LANES : (half + 1) * LANES
            ]
            rate_up = rate + rows(half_rate, up, half, start)
            rate_down = rate + rows(half_rate, down, half, start)
            if adjoint:
                rate_up = rate_up + wind
            else:
                rate_down = rate_down + wind
            depth_part = rate_up * (rows(field, up, half, start) - value) - rate_down * (
                value - rows(field, down, half, start)
            )
            row_part = (rate + rows(half_rate, slot, half, start, 1)) * (
                rows(field, slot, half, start, 1) - value
            ) - (rate + rows(half_rate, slot, half, start, -1)) * (
                value - rows(field, slot, half, start, -1)
            )
            result.append(value + depth_part + row_part + (flux[half] - flux_behind[half]))
        return result

    def save(field, grad_x, slot, start, parts):
        parts_ahead = ahead(parts)
        for half in halves:
            put(field, slot, half, start, parts[half])
            put_plain(grad_x, slot, half, start, parts_ahead[half] - parts[half])

    def source_gain(plane):
        return jnp.where(plane == source_plane[0], jnp.float32(TIME_STEP), jnp.float32(0.0))

    def source(gain, half, start):
        return gain * profile_ref[0, start : start + STRIP, half * LANES : (half + 1) * LANES]

    plane1 = index - 1

    @pl.when((plane1 >= 1) & (plane1 < total - 1))
    def _():
        slot = plane1
        gain = source_gain(plane1)
        for start in strips:
            parts = advance(state0, grad_x0, slot, start, False)
            parts = [parts[half] + source(gain, half, start) for half in halves]
            save(state1, grad_x1, slot, start, parts)

    plane2 = index - 2

    @pl.when((plane2 >= 2) & (plane2 < total - 2))
    def _():
        slot = plane2
        gain = source_gain(plane2)
        for start in strips:
            parts = advance(state1, grad_x1, slot, start, False)
            mu = []
            for half in halves:
                cols = slice(half * LANES, (half + 1) * LANES)
                state2 = parts[half] + source(gain, half, start)
                span = slice(start, start + STRIP)
                mu.append(count2[0, span, cols] * state2 - sum2[0, span, cols])
                put_plain(
                    inject1,
                    slot,
                    half,
                    start,
                    count1[0, span, cols] * rows(state1, slot, half, start) - sum1[0, span, cols],
                )
            save(adjoint2, grad_x2, slot, start, mu)

    plane3 = index - 3

    @pl.when((plane3 >= 3) & (plane3 < total - 3))
    def _():
        slot = plane3
        for start in strips:
            parts = advance(adjoint2, grad_x2, slot, start, True)
            for half in halves:
                put(
                    adjoint1,
                    slot,
                    half,
                    start,
                    parts[half] + plain(inject1, slot, half, start),
                )

    plane4 = index - 4

    def products(slot, other, half, start):
        def step(field):
            return rows(field, other, half, start) - rows(field, slot, half, start)

        return step(state0) * step(adjoint1) + step(state1) * step(adjoint2)

    @pl.when(plane4 == HALO - 1)
    def _():
        slot = plane4
        for start in strips:
            for half in halves:
                depth_product[half, start : start + STRIP, :] = products(
                    slot, slot + 1, half, start
                )

    @pl.when(plane4 >= HALO)
    def _():
        slot, up = plane4, plane4 + 1
        even = (plane4 & 1) == 0
        for start in strips:
            mu = [rows(adjoint1, slot, half, start) for half in halves]
            mu_ahead = ahead(mu)
            product_x = [
                plain(grad_x0, slot, half, start) * (mu_ahead[half] - mu[half])
                + plain(grad_x1, slot, half, start) * plain(grad_x2, slot, half, start)
                for half in halves
            ]
            product_behind = behind(product_x)
            for half in halves:
                span = slice(start, start + STRIP)
                result = product_x[half] + product_behind[half]
                upper = products(slot, up, half, start)
                result = result + (upper + depth_product[half, span, :])
                depth_product[half, span, :] = upper
                for shift in (1, -1):
                    factors = [
                        rows(field, slot, half, start, shift) - rows(field, slot, half, start)
                        for field in (state0, adjoint1, state1, adjoint2)
                    ]
                    result = result + (factors[0] * factors[1] + factors[2] * factors[3])
                result = -rows(half_rate, slot, half, start) * result
                pair_sum[half, span, :] = jnp.where(even, 0.0, pair_sum[half, span, :]) + result

    @pl.when((plane4 >= HALO) & ((plane4 & 1) == 1))
    def _():
        for half in halves:
            even_rows = pair_sum[half, pl.ds(0, size // R, R), :]
            odd_rows = pair_sum[half, pl.ds(1, size // R, R), :]
            cols = slice(half * LANES, (half + 1) * LANES)
            coarse_rows[(plane4 - HALO) >> 1, :, cols] = even_rows + odd_rows

    @pl.when(index == total - 1)
    def _():
        planes = coarse_rows.shape[0]
        for plane in range(planes):
            out_ref[pl.ds(plane, columns_table.shape[0], planes), :] = lax.dot_general(
                columns_table[...],
                coarse_rows[plane],
                (((1,), (1,)), ((), ())),
                precision=lax.Precision.HIGHEST,
                preferred_element_type=jnp.float32,
            )


def sweep(source_plane, rates, states, velocity, profile, fields):
    own, rows_count, cols_count = rates[1].shape
    total = own + 2 * HALO
    coarse = rows_count // R
    plane = (1, rows_count, cols_count)
    smem = pl.BlockSpec(memory_space=pltpu.SMEM)
    vmem = pl.BlockSpec(memory_space=pltpu.VMEM)

    def low(which):
        return pl.BlockSpec((None, *plane), lambda i: (which, jnp.minimum(i, HALO - 1), 0, 0))

    def high(which):
        return pl.BlockSpec(
            (None, *plane), lambda i: (which, jnp.clip(i - HALO - own, 0, HALO - 1), 0, 0)
        )

    middle = pl.BlockSpec(plane, lambda i: (jnp.clip(i - HALO, 0, own - 1), 0, 0))
    columns_table = jnp.asarray(np.repeat(hartley(cols_count // R), R, axis=1))
    voxels = pl.BlockSpec(
        (1, rows_count, cols_count),
        lambda i: (jnp.clip(i - HALO, 0, total - 2 * LEAD - 1), 0, 0),
    )
    def padded(kept):
        return pltpu.VMEM((kept, 2, rows_count + 2 * PAD, LANES), jnp.float32)

    def plain(kept):
        return pltpu.VMEM((kept, 2, rows_count, LANES), jnp.float32)

    return pl.pallas_call(
        sweep_kernel,
        grid=(total,),
        out_shape=jax.ShapeDtypeStruct((cols_count // R * (own // R), coarse), jnp.float32),
        in_specs=[smem, low(0), middle, high(0), low(1), middle, high(1), vmem, vmem] + [voxels] * 4 + [vmem],
        out_specs=vmem,
        scratch_shapes=[padded(LONG)] * 2
        + [padded(SHORT)] * 3
        + [plain(SHORT), plain(LONG), plain(SHORT), plain(SHORT), plain(2)]
        + [
            pltpu.VMEM((2, rows_count, LANES), jnp.float32),
            pltpu.VMEM((2, rows_count, LANES), jnp.float32),
            pltpu.VMEM((own // R, coarse, cols_count), jnp.float32),
        ],
        compiler_params=pltpu.CompilerParams(
            vmem_limit_bytes=18 * 2**20, dimension_semantics=("arbitrary",)
        ),
        cost_estimate=pl.CostEstimate(
            flops=200_000_000, bytes_accessed=34 * 2**20, transcendentals=0
        ),
        name="sweep",
    )(
        source_plane,
        *rates,
        *states,
        velocity,
        profile,
        *fields,
        columns_table,
    )


def exact_dot(a, b):
    return jnp.dot(a, b, precision=lax.Precision.HIGHEST, preferred_element_type=jnp.float32)


def filter_kernel(lam_second, received, table_ref, symbol_depth, symbol_rows, out_ref, field):
    depth_blocks, tracers, planes, size = received.shape
    for block in range(depth_blocks):
        field[block * planes : (block + 1) * planes, :] = jnp.sum(received[block], axis=0)
    table = table_ref[...]
    spectrum = exact_dot(exact_dot(table, field[...]), table)
    lam = symbol_depth[...] + symbol_rows[...] + lam_second[0]
    factor = 1.0 + PRIOR_RANGE * lam
    spectrum = spectrum * (1.0 / (factor * factor) / float(size**3))
    field[...] = exact_dot(exact_dot(table, spectrum), table)
    share = size // tracers
    group = lax.broadcasted_iota(jnp.int32, (depth_blocks, size), 1) // share
    by_plane = [field[pl.ds(plane, depth_blocks, planes), :] for plane in range(planes)]
    for tracer in range(tracers):
        part = jnp.zeros((depth_blocks, size), jnp.float32)
        for plane in range(planes):
            shift = (plane - tracer) * share % size
            moved = pltpu.roll(by_plane[plane], shift, 1) if shift else by_plane[plane]
            part = jnp.where(group == plane, moved, part)
        out_ref[pl.ds(tracer, depth_blocks, tracers), :] = part


def filtered(received, own_symbol):
    depth_blocks, tracers, planes, size = received.shape
    line = symbol(size)
    vmem = pl.BlockSpec(memory_space=pltpu.VMEM)
    return pl.pallas_call(
        filter_kernel,
        out_shape=jax.ShapeDtypeStruct((depth_blocks * tracers, size), jnp.float32),
        in_specs=[pl.BlockSpec(memory_space=pltpu.SMEM)] + [vmem] * 4,
        out_specs=vmem,
        scratch_shapes=[pltpu.VMEM((depth_blocks * planes, size), jnp.float32)],
        compiler_params=pltpu.CompilerParams(vmem_limit_bytes=16 * 2**20),
        name="filter",
    )(
        own_symbol,
        received,
        jnp.asarray(hartley(size)),
        jnp.asarray(line[:, None]),
        jnp.asarray(line[None, :]),
    )


def inverse_kernel(received, table_ref, out_ref):
    out_ref[...] = lax.dot_general(
        received[...],
        table_ref[...],
        (((0,), (0,)), ((), ())),
        precision=lax.Precision.HIGHEST,
        preferred_element_type=jnp.float32,
    )


def inverse_columns(received):
    vmem = pl.BlockSpec(memory_space=pltpu.VMEM)
    return pl.pallas_call(
        inverse_kernel,
        out_shape=jax.ShapeDtypeStruct(received.shape, jnp.float32),
        in_specs=[vmem, vmem],
        out_specs=vmem,
        compiler_params=pltpu.CompilerParams(vmem_limit_bytes=16 * 2**20),
        name="inverse_columns",
    )(received, jnp.asarray(hartley(received.shape[0])))


def edges_kernel(rate, state, first, last, sems):
    begin = rate.shape[0] - HALO
    copies = [
        pltpu.make_async_copy(source.at[pl.ds(at, HALO)], target.at[which], sems.at[which, side])
        for which, source in enumerate((rate, state))
        for side, (at, target) in enumerate(((0, first), (begin, last)))
    ]
    for copy in copies:
        copy.start()
    for copy in copies:
        copy.wait()


def edges(rate, state):
    stay = pl.BlockSpec(memory_space=pl.ANY)
    vmem = pl.BlockSpec(memory_space=pltpu.VMEM)
    end = jax.ShapeDtypeStruct((2, HALO, *rate.shape[1:]), jnp.float32)
    return pl.pallas_call(
        edges_kernel,
        out_shape=(end, end),
        in_specs=[stay, stay],
        out_specs=(vmem, vmem),
        scratch_shapes=[pltpu.SemaphoreType.DMA((2, 2))],
        compiler_params=pltpu.CompilerParams(vmem_limit_bytes=47 * 2**20),
        name="edges",
    )(rate, state)


def neighbours(first, last):
    count = lax.axis_size("domain")
    up = [(i, (i + 1) % count) for i in range(count)]
    down = [(j, i) for i, j in up]
    return lax.ppermute(last, "domain", up), lax.ppermute(first, "domain", down)


def local(log_rate, velocity, initial, profile, plane, depth, row, column, step_of, observed):
    slab, rows_count, cols_count = log_rate.shape
    domain_count, tracer_count = lax.axis_size("domain"), lax.axis_size("tracer")
    full = slab * domain_count
    offset = lax.axis_index("domain") * slab
    low, high = neighbours(*edges(log_rate, initial[0]))
    keys, values, starts, rate_near, state_near = sort_probes(
        offset.astype(jnp.int32)[None],
        depth,
        row,
        column,
        step_of,
        observed,
        slab + 2 * LEAD,
        log_rate,
        initial[0],
    )
    source_plane = (plane - (offset - HALO)) % full
    fields = bin_probes(starts, keys, values, rows_count, cols_count)
    rates = (low, rate_near, high)
    states = (low, state_near, high)
    spectral = sweep(source_plane, rates, states, velocity, profile, fields)
    first, planes, second = rows_count // R, slab // R, cols_count // R
    axes = ("domain", "tracer")
    received = lax.all_to_all(
        spectral.reshape(second, planes, first), axes, split_axis=0, concat_axis=0, tiled=True
    )
    own = lax.axis_index("domain") * tracer_count + lax.axis_index("tracer")
    own_symbol = lax.dynamic_slice(jnp.asarray(symbol(second)), (own,), (1,))
    back = filtered(received.reshape(domain_count, tracer_count, planes, first), own_symbol)
    result = lax.all_to_all(back, axes, split_axis=0, concat_axis=0, tiled=True)
    return inverse_columns(result).reshape(planes, first // tracer_count, second)


def solution(mesh):
    return jax.shard_map(
        local,
        mesh=mesh,
        in_specs=(
            P("domain", None, None),
            P(),
            P("tracer", "domain", None, None),
            P("tracer", None, None),
            P("tracer"),
            P("tracer", None),
            P("tracer", None),
            P("tracer", None),
            P("tracer", None),
            P("tracer", None),
        ),
        out_specs=P("domain", "tracer", None),
        check_vma=False,
    )
```
